128 devices in a mesh: comp: 4 (over x), tx: 4 (over y_hi, core), ty: 8 (over y_lo, z).
Axes of the slice: x: 4, y: 4 (y_hi: 2, y_lo: 2; y = y_hi * 2 + y_lo), z: 4, core: 2. Of those that a mesh axis runs over, the one named last changes fastest.
Arguments:
- model_state: float32 [4, 4, 8, 512, 2048], P('comp', None, None, 'tx', 'ty'), may hold values from -6 to 6
- sea_mask: int32 [4, 512, 2048], P('comp', 'tx', 'ty'), may hold values 0 or 1
- wave_speed: float32 [4, 8], P('comp'), may hold values from 0.1 to 0.4
- diffusivity: float32 [4, 8], P('comp'), may hold values from 0.02 to 0.2
- surface_gains: float32 [4, 3], P('comp'), may hold values from 0.1 to 0.5
- area_table: float32 [256], replicated, may hold values from 0.2 to 1
- own_cells: int32 [4, 32, 4, 2048], P('comp', ('tx', 'ty')), may hold values from 0 to 32767
- target_cells: int32 [4, 32, 4, 2048], P('comp', ('tx', 'ty')), may hold values from 0 to 32767
- weight_ids: int32 [4, 32, 4, 2048], P('comp', ('tx', 'ty')), may hold values from 0 to 255
- pair_counts: int32 [4, 32, 4], P('comp', ('tx', 'ty')), may hold values from 512 to 2048, as said below
- fold_map: int32 [512], replicated, may hold values from 0 to 511, as said below
Outputs:
- new_state: float32 [4, 4, 8, 512, 2048], P('comp', None, None, 'tx', 'ty')
The draws below stay inside these ranges and needn't reach their ends.
Inputs may be any that keep to these rules, and one draw needn't show every extreme that they name: pair_counts[g, s, n] counts the live slots that position s of component g sends to its partner n; in every component one receiving position gets 2048 from each of the positions that have it as a partner. fold_map[fold_map[x]] == x.
All inputs are finite; a program needn't handle non-finite values. No bound on the sum of `sea_mask` on one device may be relied on, other than what follows from the above.
Results may differ from the reference program's by a relative error of at most 0.0001.
Values sent between devices are 32-bit elements; how exact they have to be, the bound alone decides.
A program may use at most 192 MiB of HBM per device.

```python
import math
import jax
import jax.numpy as jnp

LEV = 8
CX = 128
CY = 256
NEAR = 4
SLOTS = 2048
AREAS = 256
NPOS = 32
ROWSTEP = 8
NX = 512
NY = 2048
N_COMP = 4
N_TX = 4
N_TY = 8


def cell_pairs(key):
    shape = (N_COMP, NPOS, NEAR, SLOTS)
    own = jax.random.randint(jax.random.fold_in(key, 101), shape, 0, CX * CY)
    row_shift = jax.random.randint(jax.random.fold_in(key, 102), shape, -2, 3)
    col_shift = jax.random.randint(jax.random.fold_in(key, 103), shape, -4, 5)
    row = jnp.clip(own // CY + row_shift, 0, CX - 1)
    col = jnp.clip(own % CY + col_shift, 0, CY - 1)
    return (own.astype(jnp.int32), (row * CY + col).astype(jnp.int32))


def draw_own_cells(key, part):
    pairs = cell_pairs(key)
    return pairs[0]


def draw_target_cells(key, part):
    pairs = cell_pairs(key)
    return pairs[1]


def draw_pair_counts(key, part):
    key = jax.random.fold_in(key, 12)
    base_counts = jax.random.randint(jax.random.fold_in(key, 1), (N_COMP, NPOS, NEAR), SLOTS // 4, SLOTS + 1)
    busiest = jax.random.randint(jax.random.fold_in(key, 2), (N_COMP, 1, 1), 0, NPOS)
    sources = jnp.arange(NPOS, dtype=jnp.int32)[None, :, None]
    partners = jnp.arange(NEAR, dtype=jnp.int32)[None, None, :]
    targets = (sources + partners % 2 + partners // 2 * ROWSTEP) % NPOS
    return jnp.where(targets == busiest, SLOTS, base_counts).astype(jnp.int32)


def draw_fold_map(key, part):
    key = jax.random.fold_in(key, 13)
    offset = jax.random.randint(key, (), 0, NX)
    return ((offset - jnp.arange(NX, dtype=jnp.int32)) % NX).astype(jnp.int32)


def set_ends(values, own_key, smallest, top_value):
    shape = values.shape
    index_at = [jax.random.randint(jax.random.fold_in(own_key, axis), (), 0, shape[axis]) for axis in range(len(shape))]
    values = values.at[tuple(index_at)].set(smallest)
    longest = shape.index(max(shape))
    index_at[longest] = (index_at[longest] + 1) % shape[longest]
    return values.at[tuple(index_at)].set(top_value)


def block_scale(rng, extent, cuts, low, top_value):
    def one(axis_at, blocks):
        steps = jax.random.uniform(jax.random.fold_in(jax.random.fold_in(rng, 6), axis_at), (blocks,), jnp.float32, low / len(cuts), top_value / len(cuts))
        return jnp.repeat(jnp.exp(steps), extent[axis_at] // blocks).reshape((-1,) + (1,) * (len(extent) - axis_at - 1))

    gain = one(*cuts[0])
    for cut in cuts[1:]:
        gain = gain * one(*cut)
    return gain


def noise(key, shape, scale, bound, pieces=(), kind=jnp.bfloat16):
    result = scale * jax.random.normal(key, shape, jnp.float32)
    if pieces:
        result = result * block_scale(key, shape, pieces, -0.22, 0.18)
    return jnp.clip(result, -bound, bound).astype(kind)


def setup_inputs(seed: int = 0) -> dict:
    key_of = jax.random.split(jax.random.key(seed), 12)
    model_state = noise(key_of[0], (N_COMP, 4, LEV, NX, NY), 1.0, 6.0, ((0, 4), (3, 4), (4, 8)), jnp.float32)
    sea_mask = set_ends((jax.random.randint(key_of[1], (N_COMP, NX, NY), 0, 10) < 7).astype(jnp.int32), jax.random.fold_in(key_of[1], 1), 0, 1)
    wave_speed = jnp.clip(jnp.exp(math.log(0.4) - 1.3862944 * jax.random.uniform(key_of[2], (N_COMP, LEV), jnp.float32) ** block_scale(key_of[2], (N_COMP, LEV), ((0, 4),), -0.2, 0.2)), 0.1, 0.4)
    diffusivity = jnp.clip(jnp.exp(math.log(0.2) - 2.3025851 * jax.random.uniform(key_of[3], (N_COMP, LEV), jnp.float32) ** block_scale(key_of[3], (N_COMP, LEV), ((0, 4),), -0.2, 0.2)), 0.02, 0.2)
    surface_gains = jnp.clip(jnp.exp(math.log(0.5) - 1.609438 * jax.random.uniform(key_of[4], (N_COMP, 3), jnp.float32) ** block_scale(key_of[4], (N_COMP, 3), ((0, 4),), -0.2, 0.2)), 0.1, 0.5)
    area_table = jnp.clip(jnp.exp(jax.random.uniform(key_of[5], (AREAS,), jnp.float32, math.log(0.2), math.log(1.0))), 0.2, 1.0)
    own_cells = draw_own_cells(jax.random.fold_in(key_of[11], 71), 0)
    target_cells = draw_target_cells(jax.random.fold_in(key_of[11], 71), 0)
    weight_ids = set_ends(jax.random.randint(key_of[8], (N_COMP, NPOS, NEAR, SLOTS), 0, AREAS), jax.random.fold_in(key_of[8], 1), 0, AREAS - 1).astype(jnp.int32)
    pair_counts = draw_pair_counts(jax.random.fold_in(key_of[11], 71), 0)
    fold_map = draw_fold_map(jax.random.fold_in(key_of[11], 71), 0)
    return {"model_state": model_state, "sea_mask": sea_mask, "wave_speed": wave_speed, "diffusivity": diffusivity, "surface_gains": surface_gains, "area_table": area_table, "own_cells": own_cells, "target_cells": target_cells, "weight_ids": weight_ids, "pair_counts": pair_counts, "fold_map": fold_map}


def to_tiles(grid):
    leading = grid.shape[:-2]
    blocks = grid.reshape(leading + (N_TX, CX, N_TY, CY))
    blocks = jnp.moveaxis(blocks, -3, -2)
    return blocks.reshape(leading + (N_TX * N_TY, CX * CY))


def from_tiles(tiled):
    leading = tiled.shape[:-2]
    blocks = tiled.reshape(leading + (N_TX, N_TY, CX, CY))
    blocks = jnp.moveaxis(blocks, -2, -3)
    return blocks.reshape(leading + (N_TX * CX, N_TY * CY))


def surface_sums(model_state, area_table, own_cells, target_cells, weight_ids, pair_counts):
    positions = N_TX * N_TY
    tile_size = CX * CY
    slot_ids = jnp.arange(SLOTS, dtype=jnp.int32)[None, None, None, :]
    living = slot_ids < pair_counts[..., None]
    weight = jnp.where(living, area_table[weight_ids], 0.0).astype(jnp.float32)
    surface = to_tiles(model_state[:, :, 0])
    groups = jnp.arange(N_COMP, dtype=jnp.int32)[:, None, None, None]
    sources = jnp.arange(positions, dtype=jnp.int32)[None, :, None, None]
    partners = jnp.arange(NEAR, dtype=jnp.int32)[None, None, :, None]
    offsets = partners % 2 + (partners // 2) * ROWSTEP
    targets = ((sources + offsets) % positions).astype(jnp.int32)
    receiver = jnp.where(groups == N_COMP - 1, slot_ids % (N_COMP - 1), N_COMP - 1).astype(jnp.int32)
    anchor = ((groups * positions + sources) * tile_size + own_cells).reshape(-1)
    placed = ((receiver * positions + targets) * tile_size + target_cells).reshape(-1)
    weight_flat = weight.reshape(-1)
    segments = N_COMP * positions * tile_size
    totals = []
    for column in (3, 1, 2):
        picked = surface[:, column].reshape(-1)[anchor]
        totals.append(jax.ops.segment_sum(weight_flat * picked, placed, segments))
    totals.append(jax.ops.segment_sum(weight_flat, placed, segments))
    stacked = jnp.stack([summed.reshape(N_COMP, positions, tile_size) for summed in totals], axis=1)
    return from_tiles(stacked)


def extend_component(fields, parity, fold_map, is_ocean):
    zero_column = jnp.zeros(fields.shape[:-2] + (1, fields.shape[-1]), jnp.float32)
    zero_row = jnp.zeros(fields.shape[:-1] + (1,), jnp.float32)
    if is_ocean:
        west_edge = fields[..., -1:, :]
        east_edge = fields[..., :1, :]
        north_edge = parity * fields[:, :, fold_map, -1][..., None]
    else:
        west_edge = zero_column
        east_edge = zero_column
        north_edge = zero_row
    middle = jnp.concatenate([zero_row, fields, north_edge], axis=-1)
    corner = jnp.zeros(fields.shape[:-2] + (1, 1), jnp.float32)
    west_edge = jnp.concatenate([corner, west_edge, corner], axis=-1)
    east_edge = jnp.concatenate([corner, east_edge, corner], axis=-1)
    return jnp.concatenate([west_edge, middle, east_edge], axis=-2)


def reference(model_state, sea_mask, wave_speed, diffusivity, surface_gains, area_table, own_cells, target_cells, weight_ids, pair_counts, fold_map):
    fluxes = surface_sums(model_state, area_table, own_cells, target_cells, weight_ids, pair_counts)
    results = []
    for component in range(N_COMP):
        is_ocean = component == N_COMP - 1
        fields = model_state[component]
        sea_cells = sea_mask[component].astype(jnp.float32)
        pressure, zonal, meridional, tracer = fields[0], fields[1], fields[2], fields[3]
        first_level = (jnp.arange(LEV, dtype=jnp.int32) == 0)[:, None, None]
        if is_ocean:
            keeping = jnp.broadcast_to(sea_cells, pressure.shape)
            tendency_mask = sea_cells
        else:
            keeping = jnp.where(first_level, 1.0 - surface_gains[component, 2] * (1.0 - sea_cells), 1.0)
            tendency_mask = jnp.ones_like(sea_cells)
        wave_factor = wave_speed[component][:, None, None]
        spread = diffusivity[component][:, None, None]
        scalars = extend_component(jnp.stack([pressure, tracer]), 1.0, fold_map, is_ocean)
        pressure_pad, tracer_pad = scalars[0], scalars[1]
        new_zonal = keeping * (zonal - 0.5 * wave_factor * (pressure_pad[:, 2:, 1:-1] - pressure_pad[:, :-2, 1:-1]))
        new_meridional = keeping * (meridional - 0.5 * wave_factor * (pressure_pad[:, 1:-1, 2:] - pressure_pad[:, 1:-1, :-2]))
        laplace = tracer_pad[:, 2:, 1:-1] + tracer_pad[:, :-2, 1:-1] + tracer_pad[:, 1:-1, 2:] + tracer_pad[:, 1:-1, :-2] - 4.0 * tracer
        new_tracer = tracer + spread * tendency_mask * laplace
        velocity = extend_component(jnp.stack([new_zonal, new_meridional]), -1.0, fold_map, is_ocean)
        divergence = velocity[0][:, 2:, 1:-1] - velocity[0][:, :-2, 1:-1] + velocity[1][:, 1:-1, 2:] - velocity[1][:, 1:-1, :-2]
        new_pressure = pressure - 0.5 * wave_factor * divergence
        heat_sum, east_sum, north_sum, area_sum = fluxes[component][0], fluxes[component][1], fluxes[component][2], fluxes[component][3]
        new_tracer = new_tracer.at[0].add(tendency_mask * surface_gains[component, 0] * (heat_sum - area_sum * tracer[0]))
        new_zonal = new_zonal.at[0].add(tendency_mask * surface_gains[component, 1] * (east_sum - area_sum * zonal[0]))
        new_meridional = new_meridional.at[0].add(tendency_mask * surface_gains[component, 1] * (north_sum - area_sum * meridional[0]))
        results.append(jnp.stack([new_pressure, new_zonal, new_meridional, new_tracer]))
    return jnp.stack(results)
```

```python
import jax
import jax.numpy as jnp
from jax import lax
from jax.experimental import pallas as pl
from jax.experimental.pallas import tpu as pltpu
from jax.sharding import PartitionSpec as P

MESH = pl.DeviceIdType.MESH
NEAR = 4
ROWS = 128
COLS = 256
GROUP = 8


def exchange_kernel(
    counts,
    state,
    mask,
    own,
    target,
    ids,
    cells_out,
    values_out,
    rows_out,
    columns_out,
    fold_out,
    fields,
    sea,
    own_v,
    target_v,
    ids_v,
    surface,
    early,
    late,
    rows_in,
    columns_in,
    load_sem,
    early_send,
    early_recv,
    late_send,
    late_recv,
    edge_send,
    edge_recv,
    fold_send,
    fold_recv,
):
    levels = fields.shape[1]
    comps = lax.axis_size("comp")
    windows = comps - 1
    count_x = lax.axis_size("tx")
    count_y = lax.axis_size("ty")
    places = count_x * count_y
    comp = lax.axis_index("comp")
    ix = lax.axis_index("tx")
    iy = lax.axis_index("ty")
    place = ix * count_y + iy
    is_ocean = comp == windows
    is_window = comp != windows
    on_fold = jnp.logical_and(is_ocean, iy == count_y - 1)
    offsets = [n % 2 + (n // 2) * count_y for n in range(NEAR)]

    def device_at(component, position):
        return (component, lax.div(position, count_y), lax.rem(position, count_y))

    loads = [
        pltpu.make_async_copy(own.at[0, 0], own_v, load_sem.at[0]),
        pltpu.make_async_copy(state.at[0, :, 0], fields.at[:, 0], load_sem.at[1]),
        pltpu.make_async_copy(target.at[0, 0], target_v, load_sem.at[2]),
        pltpu.make_async_copy(ids.at[0, 0], ids_v, load_sem.at[3]),
        pltpu.make_async_copy(
            state.at[0, :, pl.ds(1, levels - 1)], fields.at[:, pl.ds(1, levels - 1)], load_sem.at[4]
        ),
        pltpu.make_async_copy(mask.at[0], sea, load_sem.at[5]),
    ]
    for load in loads:
        load.start()

    west = (comp, lax.rem(ix + count_x - 1, count_x), iy)
    east = (comp, lax.rem(ix + 1, count_x), iy)
    south = (comp, ix, lax.rem(iy + count_y - 1, count_y))
    north = (comp, ix, lax.rem(iy + 1, count_y))

    barrier = pltpu.get_barrier_semaphore()
    for neighbour in (west, east, south, north):
        pl.semaphore_signal(barrier, inc=1, device_id=neighbour, device_id_type=MESH)
    sources = [lax.rem(place + places - offset, places) for offset in offsets]

    @pl.when(is_ocean)
    def _():
        for source in sources:
            for window in range(windows):
                pl.semaphore_signal(
                    barrier, inc=1, device_id=device_at(window, source), device_id_type=MESH
                )

    @pl.when(is_window)
    def _():
        for source in sources:
            pl.semaphore_signal(
                barrier, inc=1, device_id=device_at(windows, source), device_id_type=MESH
            )

    @pl.when(on_fold)
    def _():
        for step in range(1, count_x):
            pl.semaphore_signal(
                barrier,
                inc=1,
                device_id=(comp, lax.rem(ix + step, count_x), iy),
                device_id_type=MESH,
            )

    loads[2].wait()
    loads[3].wait()
    lane = lax.broadcasted_iota(jnp.int32, (1, COLS), 1)
    for n in range(NEAR):
        live = counts[0, 0, n]
        for row in range(GROUP):
            span = slice(row * COLS, (row + 1) * COLS)
            cell = target_v[n : n + 1, span]
            early[n, row : row + 1] = jnp.where(lane + row * COLS < live, cell, -1)
            early[n, GROUP + row : GROUP + row + 1] = ids_v[n : n + 1, span]

    @pl.when(is_window)
    def _():
        pl.semaphore_wait(barrier, 4 + NEAR)

    @pl.when(jnp.logical_and(is_ocean, iy != count_y - 1))
    def _():
        pl.semaphore_wait(barrier, 4 + windows * NEAR)

    @pl.when(on_fold)
    def _():
        pl.semaphore_wait(barrier, 4 + windows * NEAR + count_x - 1)

    slot = jnp.where(is_ocean, 0, comp * NEAR)

    def packet_copy(kind, n, window, component):
        position = lax.rem(place + offsets[n], places)
        source, target_ref, send, recv = {
            "early": (early, cells_out, early_send, early_recv),
            "late": (late, values_out, late_send, late_recv),
        }[kind]
        return pltpu.make_async_remote_copy(
            src_ref=source.at[n],
            dst_ref=target_ref.at[slot + n],
            send_sem=send.at[n * windows + window],
            recv_sem=recv.at[slot + n],
            device_id=device_at(component, position),
            device_id_type=MESH,
        )

    def send_packets(kind, n):
        @pl.when(is_ocean)
        def _():
            for window in range(windows):
                packet_copy(kind, n, window, window).start()

        @pl.when(is_window)
        def _():
            packet_copy(kind, n, 0, windows).start()

    for n in range(NEAR):
        send_packets("early", n)

    loads[0].wait()
    loads[1].wait()
    for at, variable in enumerate((3, 1, 2)):
        turned = jnp.transpose(fields[variable, 0])
        high = turned.astype(jnp.bfloat16)
        low = (turned - high.astype(jnp.float32)).astype(jnp.bfloat16)
        surface[at * COLS : (at + 1) * COLS, 0:ROWS] = high
        surface[at * COLS : (at + 1) * COLS, ROWS : 2 * ROWS] = low

    row_ids = lax.broadcasted_iota(jnp.int32, (ROWS, COLS), 0)
    col_ids = lax.broadcasted_iota(jnp.int32, (COLS, COLS), 0)

    def pick(n):
        def pick_row(row, carry):
            cell = own_v[n : n + 1, pl.ds(pl.multiple_of(row * COLS, COLS), COLS)]
            hot = jnp.where(row_ids == (cell >> 8), 1.0, 0.0).astype(jnp.bfloat16)
            chosen = jnp.dot(
                surface[...],
                jnp.concatenate([hot, hot], axis=0),
                preferred_element_type=jnp.float32,
            )
            here = col_ids == (cell & (COLS - 1))
            for at in range(3):
                part = jnp.where(here, chosen[at * COLS : (at + 1) * COLS], 0.0)
                late[n, pl.ds(at * GROUP + row, 1), :] = jnp.sum(part, axis=0, keepdims=True)
            return carry

        lax.fori_loop(0, GROUP, pick_row, 0, unroll=2)
        send_packets("late", n)

    edge_copies = []
    for at, device in enumerate((west, east)):
        edge_copies.append(
            pltpu.make_async_remote_copy(
                src_ref=rows_in.at[at],
                dst_ref=rows_out.at[1 - at],
                send_sem=edge_send.at[at],
                recv_sem=edge_recv.at[1 - at],
                device_id=device,
                device_id_type=MESH,
            )
        )
    for at, device in enumerate((south, north)):
        edge_copies.append(
            pltpu.make_async_remote_copy(
                src_ref=columns_in.at[at],
                dst_ref=columns_out.at[1 - at],
                send_sem=edge_send.at[2 + at],
                recv_sem=edge_recv.at[2 + 1 - at],
                device_id=device,
                device_id_type=MESH,
            )
        )

    def fold_copy(step):
        return pltpu.make_async_remote_copy(
            src_ref=columns_in.at[1],
            dst_ref=fold_out.at[ix],
            send_sem=fold_send.at[step],
            recv_sem=fold_recv.at[step],
            device_id=(comp, lax.rem(ix + step, count_x), iy),
            device_id_type=MESH,
        )

    fold_keep = pltpu.make_async_copy(columns_in.at[1], fold_out.at[ix], fold_send.at[0])

    def send_edges():
        loads[4].wait()
        loads[5].wait()
        for at, (near, far) in enumerate(((0, 1), (ROWS - 1, ROWS - 2))):
            for level in range(levels):
                for item, (variable, row) in enumerate(((0, near), (0, far), (1, near), (3, near))):
                    rows_in[at, item * 8 + level : item * 8 + level + 1] = fields[
                        variable, level, row : row + 1, :
                    ]
            rows_in[at, 32:33] = sea[near : near + 1].astype(jnp.float32)
        lanes = lax.broadcasted_iota(jnp.int32, (ROWS, 128), 1)
        for at, (near, far) in enumerate(((0, 1), (127, 126))):
            half = slice(at * 128, (at + 1) * 128)
            columns_in[at] = jnp.where(
                lanes == 32,
                pltpu.roll(sea[:, half].astype(jnp.float32), (32 - near) % 128, 1),
                0.0,
            )

            def add_level(level, carry):
                packed = columns_in[at]
                for item, (variable, column) in enumerate(
                    ((0, near), (0, far), (2, near), (3, near))
                ):
                    place_at = item * 8 + level
                    turned = pltpu.roll(
                        fields[variable, level, :, half],
                        lax.rem(place_at + (128 - column), 128),
                        1,
                    )
                    packed = jnp.where(lanes == place_at, turned, packed)
                columns_in[at] = packed
                return carry

            lax.fori_loop(0, levels, add_level, 0)
        for copy in edge_copies:
            copy.start()

        @pl.when(on_fold)
        def _():
            fold_keep.start()
            for step in range(1, count_x):
                fold_copy(step).start()

    pick(0)
    pick(1)
    send_edges()
    pick(2)
    pick(3)

    for copy in edge_copies:
        copy.wait_send()
        copy.wait_recv()

    @pl.when(on_fold)
    def _():
        fold_keep.wait()
        for step in range(1, count_x):
            fold_copy(step).wait_send()
            fold_copy(step).wait_recv()

    def wait_slot(kind, at):
        target_ref, recv, source = {
            "early": (cells_out, early_recv, early),
            "late": (values_out, late_recv, late),
        }[kind]
        pltpu.make_async_remote_copy(
            src_ref=source.at[0],
            dst_ref=target_ref.at[at],
            send_sem=early_send.at[0],
            recv_sem=recv.at[at],
            device_id=west,
            device_id_type=MESH,
        ).wait_recv()

    for kind in ("early", "late"):

        @pl.when(is_ocean)
        def _():
            for n in range(NEAR):
                for window in range(windows):
                    packet_copy(kind, n, window, window).wait_send()
            for at in range(windows * NEAR):
                wait_slot(kind, at)

        @pl.when(is_window)
        def _():
            for n in range(NEAR):
                packet_copy(kind, n, 0, windows).wait_send()
            for at in range(NEAR):
                wait_slot(kind, at)


def step_kernel(
    wave,
    spread,
    gains,
    state,
    mask,
    area,
    fold_map,
    cells,
    values,
    rows,
    columns,
    folded,
    result,
    fields,
    updated,
    land,
    area_v,
    fold_v,
    cells_v,
    values_v,
    rows_v,
    columns_v,
    folded_v,
    sea_v,
    row_of,
    col_of,
    addends,
    left,
    right,
    total,
    load_sem,
    level_sem,
    store_sem,
):
    levels = fields.shape[0]
    windows = lax.axis_size("comp") - 1
    count_x = lax.axis_size("tx")
    count_y = lax.axis_size("ty")
    comp = lax.axis_index("comp")
    ix = lax.axis_index("tx")
    iy = lax.axis_index("ty")
    is_ocean = comp == windows
    on_fold = jnp.logical_and(is_ocean, iy == count_y - 1)
    packets = cells_v.shape[0]

    def level_load(level):
        return pltpu.make_async_copy(state.at[0, :, level], fields.at[level], level_sem.at[level])

    def level_store(level):
        return pltpu.make_async_copy(
            updated.at[level], result.at[0, :, level], store_sem.at[level]
        )

    loads = [
        pltpu.make_async_copy(cells, cells_v, load_sem.at[0]),
        pltpu.make_async_copy(values, values_v, load_sem.at[1]),
        pltpu.make_async_copy(area, area_v, load_sem.at[2]),
        pltpu.make_async_copy(mask.at[0], sea_v, load_sem.at[3]),
        pltpu.make_async_copy(rows, rows_v, load_sem.at[4]),
        pltpu.make_async_copy(columns, columns_v, load_sem.at[5]),
        pltpu.make_async_copy(fold_map.at[pl.ds(ix * ROWS, ROWS)], fold_v, load_sem.at[6]),
    ]
    for load in loads:
        load.start()
    fold_load = pltpu.make_async_copy(folded, folded_v, load_sem.at[7])

    @pl.when(on_fold)
    def _():
        fold_load.start()

    for level in range(levels):
        level_load(level).start()
    for load in loads[:3]:
        load.wait()

    table = [
        jnp.broadcast_to(area_v[at * 128 : (at + 1) * 128][None], (GROUP, 128)) for at in range(2)
    ]
    slot_ids = lax.broadcasted_iota(
        jnp.int32, (GROUP, COLS), 0
    ) * COLS + lax.broadcasted_iota(jnp.int32, (GROUP, COLS), 1)
    mine = jnp.logical_or(slot_ids - 3 * ((slot_ids * 43691) >> 17) == comp, is_ocean)

    def prepare(at, carry):
        cell = cells_v[at, 0:GROUP]
        entry = cells_v[at, GROUP : 2 * GROUP]
        halves = []
        for half in range(2):
            index = entry[:, half * 128 : (half + 1) * 128]
            low = jnp.take_along_axis(table[0], index & 127, axis=1, mode="promise_in_bounds")
            high = jnp.take_along_axis(table[1], index & 127, axis=1, mode="promise_in_bounds")
            halves.append(jnp.where(index < 128, low, high))
        weight = jnp.concatenate(halves, axis=1)
        row = cell >> 8
        row_of[at] = row & 63
        alive = jnp.logical_and(cell >= 0, mine)
        col_of[at] = jnp.where(alive, ((row >> 6) << 8) + (cell & (COLS - 1)), -1)
        for item in range(4):
            value = weight
            if item < 3:
                value = weight * values_v[at, item * GROUP : (item + 1) * GROUP]
            high = value.astype(jnp.bfloat16).astype(jnp.float32)
            addends[at, 2 * item] = high
            addends[at, 2 * item + 1] = value - high
        return carry

    lax.fori_loop(0, jnp.where(is_ocean, packets, NEAR), prepare, 0)
    total[...] = jnp.zeros_like(total)

    for load in loads[3:]:
        load.wait()

    land[...] = 1.0 - sea_v[...].astype(jnp.float32)
    one = jnp.float32(1.0)
    zero = jnp.float32(0.0)
    valid_west = jnp.where(jnp.logical_or(is_ocean, ix > 0), one, zero)
    valid_east = jnp.where(jnp.logical_or(is_ocean, ix < count_x - 1), one, zero)
    valid_south = jnp.where(iy > 0, one, zero)
    valid_north = jnp.where(jnp.logical_or(is_ocean, iy < count_y - 1), one, zero)

    @pl.when(on_fold)
    def _():
        fold_load.wait()
        wanted = jnp.transpose(jnp.broadcast_to(fold_v[...][None], (ROWS, ROWS)))
        lanes = lax.broadcasted_iota(jnp.int32, (ROWS, 128), 1)
        gathered = jnp.zeros((ROWS, 128), jnp.float32)
        for block in range(count_x):
            hot = jnp.where(wanted == lanes + block * ROWS, 1.0, 0.0).astype(jnp.bfloat16)
            rest = folded_v[block]
            for part in range(3):
                piece = rest.astype(jnp.bfloat16)
                rest = rest - piece.astype(jnp.float32)
                gathered += jnp.dot(hot, piece, preferred_element_type=jnp.float32)
        turned = jnp.logical_and(lanes >= 16, lanes < 24)
        columns_v[1] = jnp.where(turned, -gathered, gathered)

    rows_v[0] = rows_v[0] * valid_west
    rows_v[1] = rows_v[1] * valid_east
    columns_v[0] = columns_v[0] * valid_south
    columns_v[1] = columns_v[1] * valid_north

    row_ids = lax.broadcasted_iota(jnp.int32, (ROWS, COLS), 0)
    col_ids = lax.broadcasted_iota(jnp.int32, (ROWS, COLS), 1)
    is_first_row = row_ids == 0
    is_last_row = row_ids == ROWS - 1
    is_first_col = col_ids == 0
    is_last_col = col_ids == COLS - 1
    ocean_share = jnp.where(is_ocean, one, zero)

    def before_x(field, edge):
        return jnp.where(is_first_row, edge, pltpu.roll(field, 1, 0))

    def after_x(field, edge):
        return jnp.where(is_last_row, edge, pltpu.roll(field, ROWS - 1, 0))

    def before_y(field, edge):
        return jnp.where(is_first_col, edge, pltpu.roll(field, 1, 1))

    def after_y(field, edge):
        return jnp.where(is_last_col, edge, pltpu.roll(field, COLS - 1, 1))

    def stencil(level):
        level_load(level).wait()
        pressure = fields[level, 0]
        zonal = fields[level, 1]
        meridional = fields[level, 2]
        tracer = fields[level, 3]
        half_wave = 0.5 * wave[0, level]
        drag = jnp.where(is_ocean, one, jnp.where(level == 0, gains[0, 2], zero))
        keeping = 1.0 - drag * land[...]
        tendency = 1.0 - ocean_share * land[...]
        edge_rows = [
            [rows_v[side, pl.ds(item * 8 + level, 1), :] for item in range(4)] for side in range(2)
        ]
        turn = lax.rem(128 - level, 128)
        shifted = [pltpu.roll(columns_v[side], turn, 1) for side in range(2)]
        edge_cols = [
            [shifted[side][:, item * 8 : item * 8 + 1] for item in range(4)] for side in range(2)
        ]
        row_keep = [
            (1.0 - drag * (1.0 - rows_v[0, 32:33, :])) * valid_west,
            (1.0 - drag * (1.0 - rows_v[1, 32:33, :])) * valid_east,
        ]
        col_keep = [
            (1.0 - drag * (1.0 - columns_v[0, :, 32:33])) * valid_south,
            (1.0 - drag * (1.0 - columns_v[1, :, 32:33])) * valid_north,
        ]
        new_zonal = keeping * (
            zonal
            - half_wave
            * (after_x(pressure, edge_rows[1][0]) - before_x(pressure, edge_rows[0][0]))
        )
        new_meridional = keeping * (
            meridional
            - half_wave
            * (after_y(pressure, edge_cols[1][0]) - before_y(pressure, edge_cols[0][0]))
        )
        zonal_west = row_keep[0] * (
            edge_rows[0][2] - half_wave * (pressure[0:1] - edge_rows[0][1])
        )
        zonal_east = row_keep[1] * (
            edge_rows[1][2] - half_wave * (edge_rows[1][1] - pressure[ROWS - 1 : ROWS])
        )
        meridional_south = col_keep[0] * (
            edge_cols[0][2] - half_wave * (pressure[:, 0:1] - edge_cols[0][1])
        )
        meridional_north = col_keep[1] * (
            edge_cols[1][2] - half_wave * (edge_cols[1][1] - pressure[:, COLS - 1 : COLS])
        )
        divergence = (
            after_x(new_zonal, zonal_east)
            - before_x(new_zonal, zonal_west)
            + after_y(new_meridional, meridional_north)
            - before_y(new_meridional, meridional_south)
        )
        laplace = (
            after_x(tracer, edge_rows[1][3])
            + before_x(tracer, edge_rows[0][3])
            + after_y(tracer, edge_cols[1][3])
            + before_y(tracer, edge_cols[0][3])
            - 4.0 * tracer
        )
        updated[level, 0] = pressure - half_wave * divergence
        updated[level, 1] = new_zonal
        updated[level, 2] = new_meridional
        updated[level, 3] = tracer + spread[0, level] * tendency * laplace

    narrow_ids = lax.broadcasted_iota(jnp.int32, (64, COLS), 0)
    wide_ids = lax.broadcasted_iota(jnp.int32, (2 * COLS, COLS), 0)

    def scatter(first, row):
        for at in range(4):
            span = slice(at * COLS, (at + 1) * COLS)
            here = narrow_ids == row_of[first + at, pl.ds(row, 1), :]
            for item in range(4):
                for part in range(2):
                    value = addends[first + at, 2 * item + part, pl.ds(row, 1), :]
                    lead = (part * 4 + item) * 64
                    left[lead : lead + 64, span] = jnp.where(here, value, 0.0).astype(jnp.bfloat16)
            there = wide_ids == col_of[first + at, pl.ds(row, 1), :]
            right[:, span] = jnp.where(there, 1.0, 0.0).astype(jnp.bfloat16)
        total[...] += lax.dot_general(
            left[...],
            right[...],
            (((1,), (1,)), ((), ())),
            preferred_element_type=jnp.float32,
        )

    def level_step(level, carry):
        stencil(level)
        scatter(0, level)

        @pl.when(is_ocean)
        def _():
            scatter(4, level)
            scatter(8, level)

        @pl.when(level > 0)
        def _():
            level_store(level).start()

        return carry

    lax.fori_loop(0, levels, level_step, 0)
    for row in range(levels, GROUP):
        scatter(0, row)

        @pl.when(is_ocean)
        def _():
            scatter(4, row)
            scatter(8, row)

    for half in range(2):
        span = slice(half * 64, (half + 1) * 64)
        lanes = slice(half * COLS, (half + 1) * COLS)
        sums = [
            total[item * 64 : (item + 1) * 64, lanes]
            + total[256 + item * 64 : 256 + (item + 1) * 64, lanes]
            for item in range(4)
        ]
        tendency = 1.0 - ocean_share * land[span]
        for item, variable in enumerate((3, 1, 2)):
            gain = gains[0, 0] if variable == 3 else gains[0, 1]
            updated[0, variable, span] = updated[0, variable, span] + tendency * gain * (
                sums[item] - sums[3] * fields[0, variable, span]
            )
    level_store(0).start()
    for level in range(levels):
        level_store(level).wait()


def shards(
    model_state,
    sea_mask,
    wave_speed,
    diffusivity,
    surface_gains,
    area_table,
    own_cells,
    target_cells,
    weight_ids,
    pair_counts,
    fold_map,
):
    levels = model_state.shape[2]
    windows = lax.axis_size("comp") - 1
    count_x = lax.axis_size("tx")
    packets = windows * NEAR
    anywhere = pl.BlockSpec(memory_space=pl.ANY)
    scalars = pl.BlockSpec(memory_space=pltpu.SMEM)
    f32, i32 = jnp.float32, jnp.int32
    dma = pltpu.SemaphoreType.DMA
    cells, values, rows, columns, folded = pl.pallas_call(
        exchange_kernel,
        out_shape=(
            jax.ShapeDtypeStruct((packets, 2 * GROUP, COLS), i32),
            jax.ShapeDtypeStruct((packets, 3 * GROUP, COLS), f32),
            jax.ShapeDtypeStruct((2, 40, COLS), f32),
            jax.ShapeDtypeStruct((2, ROWS, 128), f32),
            jax.ShapeDtypeStruct((count_x, ROWS, 128), f32),
        ),
        in_specs=[scalars] + [anywhere] * 5,
        out_specs=[anywhere] * 5,
        scratch_shapes=[
            pltpu.VMEM((4, levels, ROWS, COLS), f32),
            pltpu.VMEM((ROWS, COLS), i32),
            pltpu.VMEM((NEAR, GROUP * COLS), i32),
            pltpu.VMEM((NEAR, GROUP * COLS), i32),
            pltpu.VMEM((NEAR, GROUP * COLS), i32),
            pltpu.VMEM((3 * COLS, 2 * ROWS), jnp.bfloat16),
            pltpu.VMEM((NEAR, 2 * GROUP, COLS), i32),
            pltpu.VMEM((NEAR, 3 * GROUP, COLS), f32),
            pltpu.VMEM((2, 40, COLS), f32),
            pltpu.VMEM((2, ROWS, 128), f32),
            dma((6,)),
            dma((packets,)),
            dma((packets,)),
            dma((packets,)),
            dma((packets,)),
            dma((4,)),
            dma((4,)),
            dma((count_x,)),
            dma((count_x,)),
        ],
        compiler_params=pltpu.CompilerParams(
            collective_id=0, has_side_effects=True, vmem_limit_bytes=32 * 2**20
        ),
        name="exchange",
    )(pair_counts, model_state, sea_mask, own_cells, target_cells, weight_ids)
    return pl.pallas_call(
        step_kernel,
        out_shape=jax.ShapeDtypeStruct(model_state.shape, f32),
        in_specs=[scalars] * 3 + [anywhere] * 9,
        out_specs=anywhere,
        scratch_shapes=[
            pltpu.VMEM((levels, 4, ROWS, COLS), f32),
            pltpu.VMEM((levels, 4, ROWS, COLS), f32),
            pltpu.VMEM((ROWS, COLS), f32),
            pltpu.VMEM(area_table.shape, f32),
            pltpu.VMEM((ROWS,), i32),
            pltpu.VMEM(cells.shape, i32),
            pltpu.VMEM(values.shape, f32),
            pltpu.VMEM(rows.shape, f32),
            pltpu.VMEM(columns.shape, f32),
            pltpu.VMEM(folded.shape, f32),
            pltpu.VMEM((ROWS, COLS), i32),
            pltpu.VMEM((packets, GROUP, COLS), i32),
            pltpu.VMEM((packets, GROUP, COLS), i32),
            pltpu.VMEM((packets, 8, GROUP, COLS), f32),
            pltpu.VMEM((2 * 4 * 64, 4 * COLS), jnp.bfloat16),
            pltpu.VMEM((2 * COLS, 4 * COLS), jnp.bfloat16),
            pltpu.VMEM((2 * 4 * 64, 2 * COLS), f32),
            dma((8,)),
            dma((levels,)),
            dma((levels,)),
        ],
        compiler_params=pltpu.CompilerParams(vmem_limit_bytes=48 * 2**20),
        name="step",
    )(
        wave_speed,
        diffusivity,
        surface_gains,
        model_state,
        sea_mask,
        area_table,
        fold_map,
        cells,
        values,
        rows,
        columns,
        folded,
    )


def solution(mesh):
    in_specs = (
        P("comp", None, None, "tx", "ty"),
        P("comp", "tx", "ty"),
        P("comp", None),
        P("comp", None),
        P("comp", None),
        P(),
        P("comp", ("tx", "ty"), None, None),
        P("comp", ("tx", "ty"), None, None),
        P("comp", ("tx", "ty"), None, None),
        P("comp", ("tx", "ty"), None),
        P(),
    )
    out_specs = P("comp", None, None, "tx", "ty")
    return jax.shard_map(shards, mesh=mesh, in_specs=in_specs, out_specs=out_specs, check_vma=False)
```

```python
import jax
import jax.numpy as jnp
from jax import lax
from jax.experimental import pallas as pl
from jax.experimental.pallas import tpu as pltpu
from jax.sharding import PartitionSpec as P

MESH = pl.DeviceIdType.MESH
NEAR = 4
ROWS = 128
COLS = 256
f32 = jnp.float32
i32 = jnp.int32
f8 = jnp.float8_e4m3fn
dma = pltpu.SemaphoreType.DMA
GROUP = 8
BATCH = 8


def exchange_kernel(
    counts,
    state,
    mask,
    own,
    target,
    ids,
    area,
    fold_map,
    places_out,
    weights_out,
    live_out,
    values_out,
    rows_out,
    columns_out,
    fields,
    sea,
    own_v,
    target_v,
    ids_v,
    area_v,
    fold_v,
    surface,
    early,
    late,
    rows_in,
    columns_in,
    arrived,
    places,
    weights,
    live,
    rows_got,
    columns_got,
    fold_got,
    load_sem,
    store_sem,
    early_send,
    early_recv,
    late_send,
    late_recv,
    edge_send,
    edge_recv,
    fold_send,
    fold_recv,
):
    levels = fields.shape[1]
    comps = lax.axis_size("comp")
    windows = comps - 1
    count_x = lax.axis_size("tx")
    count_y = lax.axis_size("ty")
    positions = count_x * count_y
    comp = lax.axis_index("comp")
    ix = lax.axis_index("tx")
    iy = lax.axis_index("ty")
    place = ix * count_y + iy
    is_ocean = comp == windows
    is_window = comp != windows
    on_fold = jnp.logical_and(is_ocean, iy == count_y - 1)
    offsets = [n % 2 + (n // 2) * count_y for n in range(NEAR)]

    def device_at(component, position):
        return (component, lax.div(position, count_y), lax.rem(position, count_y))

    loads = [
        pltpu.make_async_copy(target.at[0, 0], target_v, load_sem.at[0]),
        pltpu.make_async_copy(ids.at[0, 0], ids_v, load_sem.at[1]),
        pltpu.make_async_copy(own.at[0, 0], own_v, load_sem.at[2]),
        pltpu.make_async_copy(state.at[0, :, 0], fields.at[:, 0], load_sem.at[3]),
        pltpu.make_async_copy(
            state.at[0, :, pl.ds(1, levels - 1)], fields.at[:, pl.ds(1, levels - 1)], load_sem.at[4]
        ),
        pltpu.make_async_copy(mask.at[0], sea, load_sem.at[5]),
        pltpu.make_async_copy(area, area_v, load_sem.at[6]),
        pltpu.make_async_copy(fold_map.at[pl.ds(ix * ROWS, ROWS)], fold_v, load_sem.at[7]),
    ]
    for load in loads:
        load.start()

    west = (comp, lax.rem(ix + count_x - 1, count_x), iy)
    east = (comp, lax.rem(ix + 1, count_x), iy)
    south = (comp, ix, lax.rem(iy + count_y - 1, count_y))
    north = (comp, ix, lax.rem(iy + 1, count_y))

    barrier = pltpu.get_barrier_semaphore()
    for neighbour in (west, east, south, north):
        pl.semaphore_signal(barrier, inc=1, device_id=neighbour, device_id_type=MESH)
    sources = [lax.rem(place + positions - offset, positions) for offset in offsets]

    @pl.when(is_ocean)
    def _():
        for source in sources:
            for window in range(windows):
                pl.semaphore_signal(
                    barrier, inc=1, device_id=device_at(window, source), device_id_type=MESH
                )

    @pl.when(is_window)
    def _():
        for source in sources:
            pl.semaphore_signal(
                barrier, inc=1, device_id=device_at(windows, source), device_id_type=MESH
            )

    @pl.when(on_fold)
    def _():
        for step in range(1, count_x):
            pl.semaphore_signal(
                barrier,
                inc=1,
                device_id=(comp, lax.rem(ix + step, count_x), iy),
                device_id_type=MESH,
            )

    loads[0].wait()
    loads[1].wait()
    lane = lax.broadcasted_iota(jnp.int32, (1, COLS), 1)
    for n in range(NEAR):
        limit = counts[0, 0, n]
        for row in range(GROUP):
            span = slice(row * COLS, (row + 1) * COLS)
            cell = target_v[n : n + 1, span]
            early[n, row : row + 1] = jnp.where(lane + row * COLS < limit, cell, -1)
            early[n, GROUP + row : GROUP + row + 1] = ids_v[n : n + 1, span]

    slot = jnp.where(is_ocean, 0, comp * NEAR)

    def packet_copy(kind, n, window, component):
        position = lax.rem(place + offsets[n], positions)
        source, target_ref, send, recv = {
            "early": (early, arrived, early_send, early_recv),
            "late": (late, values_out, late_send, late_recv),
        }[kind]
        return pltpu.make_async_remote_copy(
            src_ref=source.at[n],
            dst_ref=target_ref.at[slot + n],
            send_sem=send.at[n * windows + window],
            recv_sem=recv.at[slot + n],
            device_id=device_at(component, position),
            device_id_type=MESH,
        )

    def send_packets(kind, n):
        @pl.when(is_ocean)
        def _():
            for window in range(windows):
                packet_copy(kind, n, window, window).start()

        @pl.when(is_window)
        def _():
            packet_copy(kind, n, 0, windows).start()

    @pl.when(is_window)
    def _():
        pl.semaphore_wait(barrier, 4 + NEAR)

    @pl.when(jnp.logical_and(is_ocean, iy != count_y - 1))
    def _():
        pl.semaphore_wait(barrier, 4 + windows * NEAR)

    @pl.when(on_fold)
    def _():
        pl.semaphore_wait(barrier, 4 + windows * NEAR + count_x - 1)

    for n in range(NEAR):
        send_packets("early", n)

    loads[2].wait()
    loads[3].wait()
    for at, variable in enumerate((3, 1, 2)):
        turned = jnp.transpose(fields[variable, 0])
        high = turned.astype(jnp.bfloat16)
        low = (turned - high.astype(jnp.float32)).astype(jnp.bfloat16)
        surface[at * COLS : (at + 1) * COLS, 0:ROWS] = high
        surface[at * COLS : (at + 1) * COLS, ROWS : 2 * ROWS] = low

    row_ids = lax.broadcasted_iota(jnp.int32, (ROWS, COLS), 0)
    col_ids = lax.broadcasted_iota(jnp.int32, (COLS, COLS), 0)

    def pick(n):
        def pick_row(row, carry):
            cell = own_v[n : n + 1, pl.ds(pl.multiple_of(row * COLS, COLS), COLS)]
            hot = jnp.where(row_ids == (cell >> 8), 1.0, 0.0).astype(jnp.bfloat16)
            chosen = jnp.dot(
                surface[...],
                jnp.concatenate([hot, hot], axis=0),
                preferred_element_type=jnp.float32,
            )
            here = col_ids == (cell & (COLS - 1))
            for at in range(3):
                part = jnp.where(here, chosen[at * COLS : (at + 1) * COLS], 0.0)
                late[n, pl.ds(at * GROUP + row, 1), :] = jnp.sum(part, axis=0, keepdims=True)
            return carry

        lax.fori_loop(0, GROUP, pick_row, 0, unroll=8)

    edge_copies = []
    for at, device in enumerate((west, east)):
        edge_copies.append(
            pltpu.make_async_remote_copy(
                src_ref=rows_in.at[at],
                dst_ref=rows_got.at[1 - at],
                send_sem=edge_send.at[at],
                recv_sem=edge_recv.at[1 - at],
                device_id=device,
                device_id_type=MESH,
            )
        )
    for at, device in enumerate((south, north)):
        edge_copies.append(
            pltpu.make_async_remote_copy(
                src_ref=columns_in.at[at],
                dst_ref=columns_got.at[1 - at],
                send_sem=edge_send.at[2 + at],
                recv_sem=edge_recv.at[2 + 1 - at],
                device_id=device,
                device_id_type=MESH,
            )
        )

    def fold_copy(step):
        return pltpu.make_async_remote_copy(
            src_ref=columns_in.at[1],
            dst_ref=fold_got.at[ix],
            send_sem=fold_send.at[step],
            recv_sem=fold_recv.at[step],
            device_id=(comp, lax.rem(ix + step, count_x), iy),
            device_id_type=MESH,
        )

    fold_keep = pltpu.make_async_copy(columns_in.at[1], fold_got.at[ix], fold_send.at[0])

    def send_edges():
        loads[4].wait()
        loads[5].wait()
        for at, (near, far) in enumerate(((0, 1), (ROWS - 1, ROWS - 2))):
            for level in range(levels):
                for item, (variable, row) in enumerate(((0, near), (0, far), (1, near), (3, near))):
                    rows_in[at, item * 8 + level : item * 8 + level + 1] = fields[
                        variable, level, row : row + 1, :
                    ]
            rows_in[at, 32:33] = sea[near : near + 1].astype(jnp.float32)
        lanes = lax.broadcasted_iota(jnp.int32, (ROWS, 128), 1)
        for at, (near, far) in enumerate(((0, 1), (127, 126))):
            half = slice(at * 128, (at + 1) * 128)
            columns_in[at] = jnp.where(
                lanes == 32,
                pltpu.roll(sea[:, half].astype(jnp.float32), (32 - near) % 128, 1),
                0.0,
            )

            def add_level(level, carry):
                packed = columns_in[at]
                for item, (variable, column) in enumerate(
                    ((0, near), (0, far), (2, near), (3, near))
                ):
                    place_at = item * 8 + level
                    turned = pltpu.roll(
                        fields[variable, level, :, half],
                        lax.rem(place_at + (128 - column), 128),
                        1,
                    )
                    packed = jnp.where(lanes == place_at, turned, packed)
                columns_in[at] = packed
                return carry

            lax.fori_loop(0, levels, add_level, 0, unroll=2)
        for copy in edge_copies:
            copy.start()

        @pl.when(on_fold)
        def _():
            fold_keep.start()
            for step in range(1, count_x):
                fold_copy(step).start()

    pick(0)
    send_packets("late", 0)
    for n in range(1, NEAR):
        pick(n)
        send_packets("late", n)
    send_edges()

    def wait_slot(kind, at):
        target_ref, recv, source = {
            "early": (arrived, early_recv, early),
            "late": (values_out, late_recv, late),
        }[kind]
        pltpu.make_async_remote_copy(
            src_ref=source.at[0],
            dst_ref=target_ref.at[at],
            send_sem=early_send.at[0],
            recv_sem=recv.at[at],
            device_id=west,
            device_id_type=MESH,
        ).wait_recv()

    def finish(kind):
        @pl.when(is_ocean)
        def _():
            for n in range(NEAR):
                for window in range(windows):
                    packet_copy(kind, n, window, window).wait_send()
            for at in range(windows * NEAR):
                wait_slot(kind, at)

        @pl.when(is_window)
        def _():
            for n in range(NEAR):
                packet_copy(kind, n, 0, windows).wait_send()
            for at in range(NEAR):
                wait_slot(kind, at)

    loads[6].wait()
    loads[7].wait()
    spare = windows * NEAR * GROUP
    places[0, spare : spare + GROUP] = jnp.zeros((GROUP, COLS), i32)
    places[1, spare : spare + GROUP] = jnp.full((GROUP, COLS), -1, i32)
    table = [
        jnp.broadcast_to(area_v[at * 128 : (at + 1) * 128][None], (GROUP, 128)) for at in range(2)
    ]
    slot_ids = lax.broadcasted_iota(
        jnp.int32, (GROUP, COLS), 0
    ) * COLS + lax.broadcasted_iota(jnp.int32, (GROUP, COLS), 1)
    mine = jnp.logical_or(slot_ids - 3 * ((slot_ids * 43691) >> 17) == comp, is_ocean)
    finish("early")

    def place_packets(group, carry):
        for n in range(NEAR):
            at = group * NEAR + n
            cell = arrived[at, 0:GROUP]
            entry = arrived[at, GROUP : 2 * GROUP]
            lines = pl.ds(pl.multiple_of(at * GROUP, GROUP), GROUP)
            for half in range(2):
                span = slice(half * 128, (half + 1) * 128)
                index = entry[:, span]
                low = jnp.take_along_axis(table[0], index & 127, axis=1, mode="promise_in_bounds")
                high = jnp.take_along_axis(table[1], index & 127, axis=1, mode="promise_in_bounds")
                weights[lines, span] = jnp.where(index < 128, low, high)
            row = cell >> 8
            places[0, lines] = row & 63
            alive = jnp.logical_and(cell >= 0, mine)
            places[1, lines] = jnp.where(alive, ((row >> 6) << 8) + (cell & (COLS - 1)), -1)
            used = jnp.sum(jnp.where(cell >= 0, 1.0, 0.0), axis=0, keepdims=True)
            used = jnp.sum(used, axis=1, keepdims=True)
            live[pl.ds(at, 1)] = jnp.broadcast_to(used, (1, 128)).astype(jnp.int32)
        return carry

    lax.fori_loop(0, jnp.where(is_ocean, windows, 1), place_packets, 0)
    stores = [
        pltpu.make_async_copy(places, places_out, store_sem.at[0]),
        pltpu.make_async_copy(weights, weights_out, store_sem.at[1]),
        pltpu.make_async_copy(live, live_out, store_sem.at[2]),
        pltpu.make_async_copy(rows_got, rows_out, store_sem.at[3]),
        pltpu.make_async_copy(columns_got, columns_out, store_sem.at[4]),
    ]
    for store in stores[:3]:
        store.start()

    for copy in edge_copies:
        copy.wait_send()
        copy.wait_recv()
    one = jnp.float32(1.0)
    zero = jnp.float32(0.0)
    rows_got[0] = rows_got[0] * jnp.where(jnp.logical_or(is_ocean, ix > 0), one, zero)
    rows_got[1] = rows_got[1] * jnp.where(jnp.logical_or(is_ocean, ix < count_x - 1), one, zero)
    columns_got[0] = columns_got[0] * jnp.where(iy > 0, one, zero)
    columns_got[1] = columns_got[1] * jnp.where(iy < count_y - 1, one, zero)

    @pl.when(on_fold)
    def _():
        fold_keep.wait()
        for step in range(1, count_x):
            fold_copy(step).wait_send()
            fold_copy(step).wait_recv()
        wanted = jnp.transpose(jnp.broadcast_to(fold_v[...][None], (ROWS, ROWS)))
        lanes = lax.broadcasted_iota(jnp.int32, (ROWS, 128), 1)
        gathered = jnp.zeros((ROWS, 128), f32)
        for block in range(count_x):
            hot = jnp.where(wanted == lanes + block * ROWS, 1.0, 0.0).astype(jnp.bfloat16)
            rest = fold_got[block]
            for part in range(3):
                piece = rest.astype(jnp.bfloat16)
                rest = rest - piece.astype(f32)
                gathered += jnp.dot(hot, piece, preferred_element_type=f32)
        turned = jnp.logical_and(lanes >= 16, lanes < 24)
        columns_got[1] = jnp.where(turned, -gathered, gathered)

    for store in stores[3:]:
        store.start()
    finish("late")
    for store in stores:
        store.wait()


def step_kernel(
    wave,
    spread,
    gains,
    state,
    mask,
    places,
    weights,
    live,
    values,
    rows,
    columns,
    result,
    fields,
    updated,
    land,
    places_v,
    weights_v,
    values_v,
    rows_v,
    columns_v,
    sea_v,
    addends,
    live_s,
    order,
    left,
    right,
    total,
    load_sem,
    level_sem,
    store_sem,
):
    levels = fields.shape[0]
    windows = lax.axis_size("comp") - 1
    count_x = lax.axis_size("tx")
    count_y = lax.axis_size("ty")
    comp = lax.axis_index("comp")
    ix = lax.axis_index("tx")
    iy = lax.axis_index("ty")
    is_ocean = comp == windows
    packets = values_v.shape[0]

    def level_load(level):
        return pltpu.make_async_copy(state.at[0, :, level], fields.at[level], level_sem.at[level])

    def level_store(level):
        return pltpu.make_async_copy(
            updated.at[level], result.at[0, :, level], store_sem.at[level]
        )

    loads = [
        pltpu.make_async_copy(live, live_s, load_sem.at[0]),
        pltpu.make_async_copy(values, values_v, load_sem.at[1]),
        pltpu.make_async_copy(weights, weights_v, load_sem.at[2]),
        pltpu.make_async_copy(places, places_v, load_sem.at[3]),
        pltpu.make_async_copy(mask.at[0], sea_v, load_sem.at[4]),
        pltpu.make_async_copy(rows, rows_v, load_sem.at[5]),
        pltpu.make_async_copy(columns, columns_v, load_sem.at[6]),
    ]
    for load in loads:
        load.start()
    for level in range(levels):
        level_load(level).start()

    spare = packets * GROUP
    addends[:, spare : spare + GROUP] = jnp.zeros((12, GROUP, COLS), f32)
    total[...] = jnp.zeros_like(total)
    for at in range(spare + GROUP):
        order[at] = spare
    loads[0].wait()

    def list_packet(at, count):
        lines = (live_s[at, 0] + COLS - 1) // COLS

        def list_row(row, carry):
            order[count + row] = at * GROUP + row
            return carry

        lax.fori_loop(0, lines, list_row, 0)
        return count + lines

    live_lines = lax.fori_loop(0, jnp.where(is_ocean, packets, NEAR), list_packet, 0)

    for load in loads[1:]:
        load.wait()

    def split_packets(group, carry):
        for n in range(NEAR):
            at = group * NEAR + n
            lines = pl.ds(pl.multiple_of(at * GROUP, GROUP), GROUP)
            weight = weights_v[lines] * 64.0
            for item in range(4):
                value = weight
                if item < 3:
                    value = weight * values_v[at, item * GROUP : (item + 1) * GROUP]
                for part in range(3):
                    piece = value.astype(f8).astype(f32)
                    addends[part * 4 + item, lines] = piece
                    value = (value - piece) * 16.0
        return carry

    lax.fori_loop(0, jnp.where(is_ocean, packets // NEAR, 1), split_packets, 0)
    land[...] = 1.0 - sea_v[...].astype(jnp.float32)
    one = jnp.float32(1.0)
    zero = jnp.float32(0.0)
    valid_west = jnp.where(jnp.logical_or(is_ocean, ix > 0), one, zero)
    valid_east = jnp.where(jnp.logical_or(is_ocean, ix < count_x - 1), one, zero)
    valid_south = jnp.where(iy > 0, one, zero)
    valid_north = jnp.where(jnp.logical_or(is_ocean, iy < count_y - 1), one, zero)

    row_ids = lax.broadcasted_iota(jnp.int32, (ROWS, COLS), 0)
    col_ids = lax.broadcasted_iota(jnp.int32, (ROWS, COLS), 1)
    is_first_row = row_ids == 0
    is_last_row = row_ids == ROWS - 1
    is_first_col = col_ids == 0
    is_last_col = col_ids == COLS - 1
    ocean_share = jnp.where(is_ocean, one, zero)

    def before_x(field, edge):
        return jnp.where(is_first_row, edge, pltpu.roll(field, 1, 0))

    def after_x(field, edge):
        return jnp.where(is_last_row, edge, pltpu.roll(field, ROWS - 1, 0))

    def before_y(field, edge):
        return jnp.where(is_first_col, edge, pltpu.roll(field, 1, 1))

    def after_y(field, edge):
        return jnp.where(is_last_col, edge, pltpu.roll(field, COLS - 1, 1))

    def stencil(level):
        level_load(level).wait()
        pressure = fields[level, 0]
        zonal = fields[level, 1]
        meridional = fields[level, 2]
        tracer = fields[level, 3]
        half_wave = 0.5 * wave[0, level]
        drag = jnp.where(is_ocean, one, jnp.where(level == 0, gains[0, 2], zero))
        keeping = 1.0 - drag * land[...]
        tendency = 1.0 - ocean_share * land[...]
        edge_rows = [
            [rows_v[side, pl.ds(item * 8 + level, 1), :] for item in range(4)] for side in range(2)
        ]
        turn = lax.rem(128 - level, 128)
        shifted = [pltpu.roll(columns_v[side], turn, 1) for side in range(2)]
        edge_cols = [
            [shifted[side][:, item * 8 : item * 8 + 1] for item in range(4)] for side in range(2)
        ]
        row_keep = [
            (1.0 - drag * (1.0 - rows_v[0, 32:33, :])) * valid_west,
            (1.0 - drag * (1.0 - rows_v[1, 32:33, :])) * valid_east,
        ]
        col_keep = [
            (1.0 - drag * (1.0 - columns_v[0, :, 32:33])) * valid_south,
            (1.0 - drag * (1.0 - columns_v[1, :, 32:33])) * valid_north,
        ]
        new_zonal = keeping * (
            zonal
            - half_wave
            * (after_x(pressure, edge_rows[1][0]) - before_x(pressure, edge_rows[0][0]))
        )
        new_meridional = keeping * (
            meridional
            - half_wave
            * (after_y(pressure, edge_cols[1][0]) - before_y(pressure, edge_cols[0][0]))
        )
        zonal_west = row_keep[0] * (
            edge_rows[0][2] - half_wave * (pressure[0:1] - edge_rows[0][1])
        )
        zonal_east = row_keep[1] * (
            edge_rows[1][2] - half_wave * (edge_rows[1][1] - pressure[ROWS - 1 : ROWS])
        )
        meridional_south = col_keep[0] * (
            edge_cols[0][2] - half_wave * (pressure[:, 0:1] - edge_cols[0][1])
        )
        meridional_north = col_keep[1] * (
            edge_cols[1][2] - half_wave * (edge_cols[1][1] - pressure[:, COLS - 1 : COLS])
        )
        divergence = (
            after_x(new_zonal, zonal_east)
            - before_x(new_zonal, zonal_west)
            + after_y(new_meridional, meridional_north)
            - before_y(new_meridional, meridional_south)
        )
        laplace = (
            after_x(tracer, edge_rows[1][3])
            + before_x(tracer, edge_rows[0][3])
            + after_y(tracer, edge_cols[1][3])
            + before_y(tracer, edge_cols[0][3])
            - 4.0 * tracer
        )
        updated[level, 0] = pressure - half_wave * divergence
        updated[level, 1] = new_zonal
        updated[level, 2] = new_meridional
        updated[level, 3] = tracer + spread[0, level] * tendency * laplace

    narrow_ids = lax.broadcasted_iota(jnp.int16, (64, COLS), 0)
    wide_ids = lax.broadcasted_iota(jnp.int16, (2 * COLS, COLS), 0)
    one16 = jnp.ones((), jnp.bfloat16)
    zero16 = jnp.zeros((), jnp.bfloat16)

    def repeated(line, count, kind):
        tile = jnp.broadcast_to(line, (16, COLS)).astype(kind)
        return jnp.concatenate([tile] * (count // 16), axis=0)

    def scatter(batch):
        for at in range(BATCH):
            line = pl.ds(order[batch * BATCH + at], 1)
            span = slice(at * COLS, (at + 1) * COLS)
            here = narrow_ids == repeated(places_v[0, line, :], 64, jnp.int16)
            for item in range(4):
                for part in range(3):
                    value = addends[part * 4 + item, line, :]
                    lead = (part * 4 + item) * 64
                    left[lead : lead + 64, span] = jnp.where(
                        here, repeated(value, 64, jnp.bfloat16), zero16
                    ).astype(f8)
            there = wide_ids == repeated(places_v[1, line, :], 2 * COLS, jnp.int16)
            right[:, span] = jnp.where(there, one16, zero16).astype(f8)
        total[...] += lax.dot_general(
            left[...],
            right[...],
            (((1,), (1,)), ((), ())),
            preferred_element_type=jnp.float32,
        )

    def level_step(level, carry):
        stencil(level)
        scatter(level)

        @pl.when(level > 0)
        def _():
            level_store(level).start()

        return carry

    lax.fori_loop(0, levels, level_step, 0)

    def extra_step(batch, carry):
        scatter(batch)
        return carry

    lax.fori_loop(levels, jnp.maximum(levels, (live_lines + BATCH - 1) // BATCH), extra_step, 0)

    for half in range(2):
        span = slice(half * 64, (half + 1) * 64)
        lanes = slice(half * COLS, (half + 1) * COLS)
        sums = [
            total[item * 64 : (item + 1) * 64, lanes] * (1.0 / 64.0)
            + total[256 + item * 64 : 256 + (item + 1) * 64, lanes] * (1.0 / 1024.0)
            + total[512 + item * 64 : 512 + (item + 1) * 64, lanes] * (1.0 / 16384.0)
            for item in range(4)
        ]
        tendency = 1.0 - ocean_share * land[span]
        for item, variable in enumerate((3, 1, 2)):
            gain = gains[0, 0] if variable == 3 else gains[0, 1]
            updated[0, variable, span] = updated[0, variable, span] + tendency * gain * (
                sums[item] - sums[3] * fields[0, variable, span]
            )
    level_store(0).start()
    for level in range(levels):
        level_store(level).wait()


def exchange_call(
    model_state, sea_mask, own_cells, target_cells, weight_ids, pair_counts, area_table, fold_map
):
    levels = model_state.shape[2]
    packets = (lax.axis_size("comp") - 1) * NEAR
    lines = packets * GROUP
    count_x = lax.axis_size("tx")
    anywhere = pl.BlockSpec(memory_space=pl.ANY)
    shapes = [
        ((2, lines + GROUP, COLS), i32),
        ((lines, COLS), f32),
        ((16, 128), i32),
        ((packets, 3 * GROUP, COLS), f32),
        ((2, 40, COLS), f32),
        ((2, ROWS, 128), f32),
    ]
    return pl.pallas_call(
        exchange_kernel,
        out_shape=tuple(jax.ShapeDtypeStruct(shape, kind) for shape, kind in shapes),
        in_specs=[pl.BlockSpec(memory_space=pltpu.SMEM)] + [anywhere] * 7,
        out_specs=[anywhere] * 6,
        scratch_shapes=[
            pltpu.VMEM((4, levels, ROWS, COLS), f32),
            pltpu.VMEM((ROWS, COLS), i32),
            pltpu.VMEM((NEAR, GROUP * COLS), i32),
            pltpu.VMEM((NEAR, GROUP * COLS), i32),
            pltpu.VMEM((NEAR, GROUP * COLS), i32),
            pltpu.VMEM(area_table.shape, f32),
            pltpu.VMEM((ROWS,), i32),
            pltpu.VMEM((3 * COLS, 2 * ROWS), jnp.bfloat16),
            pltpu.VMEM((NEAR, 2 * GROUP, COLS), i32),
            pltpu.VMEM((NEAR, 3 * GROUP, COLS), f32),
            pltpu.VMEM((2, 40, COLS), f32),
            pltpu.VMEM((2, ROWS, 128), f32),
            pltpu.VMEM((packets, 2 * GROUP, COLS), i32),
            pltpu.VMEM((2, lines + GROUP, COLS), i32),
            pltpu.VMEM((lines, COLS), f32),
            pltpu.VMEM((16, 128), i32),
            pltpu.VMEM((2, 40, COLS), f32),
            pltpu.VMEM((2, ROWS, 128), f32),
            pltpu.VMEM((count_x, ROWS, 128), f32),
            dma((8,)),
            dma((5,)),
            dma((packets,)),
            dma((packets,)),
            dma((packets,)),
            dma((packets,)),
            dma((4,)),
            dma((4,)),
            dma((count_x,)),
            dma((count_x,)),
        ],
        compiler_params=pltpu.CompilerParams(
            collective_id=0, has_side_effects=True, vmem_limit_bytes=60 * 2**20
        ),
        name="exchange",
    )(
        pair_counts,
        model_state,
        sea_mask,
        own_cells,
        target_cells,
        weight_ids,
        area_table,
        fold_map,
    )


def step_call(
    model_state,
    sea_mask,
    wave_speed,
    diffusivity,
    surface_gains,
    places,
    weights,
    live,
    values,
    rows,
    columns,
):
    levels = model_state.shape[2]
    lines = places.shape[1]
    anywhere = pl.BlockSpec(memory_space=pl.ANY)
    scalars = pl.BlockSpec(memory_space=pltpu.SMEM)
    return pl.pallas_call(
        step_kernel,
        out_shape=jax.ShapeDtypeStruct(model_state.shape, f32),
        in_specs=[scalars] * 3 + [anywhere] * 8,
        out_specs=anywhere,
        scratch_shapes=[
            pltpu.VMEM((levels, 4, ROWS, COLS), f32),
            pltpu.VMEM((levels, 4, ROWS, COLS), f32),
            pltpu.VMEM((ROWS, COLS), f32),
            pltpu.VMEM(places.shape, i32),
            pltpu.VMEM(weights.shape, f32),
            pltpu.VMEM(values.shape, f32),
            pltpu.VMEM(rows.shape, f32),
            pltpu.VMEM(columns.shape, f32),
            pltpu.VMEM((ROWS, COLS), i32),
            pltpu.VMEM((12, lines, COLS), f32),
            pltpu.SMEM(live.shape, i32),
            pltpu.SMEM((lines,), i32),
            pltpu.VMEM((3 * 4 * 64, BATCH * COLS), f8),
            pltpu.VMEM((2 * COLS, BATCH * COLS), f8),
            pltpu.VMEM((3 * 4 * 64, 2 * COLS), f32),
            dma((7,)),
            dma((levels,)),
            dma((levels,)),
        ],
        compiler_params=pltpu.CompilerParams(vmem_limit_bytes=60 * 2**20),
        name="step",
    )(
        wave_speed,
        diffusivity,
        surface_gains,
        model_state,
        sea_mask,
        places,
        weights,
        live,
        values,
        rows,
        columns,
    )


def shards(
    model_state,
    sea_mask,
    wave_speed,
    diffusivity,
    surface_gains,
    area_table,
    own_cells,
    target_cells,
    weight_ids,
    pair_counts,
    fold_map,
):
    exchanged = exchange_call(
        model_state,
        sea_mask,
        own_cells,
        target_cells,
        weight_ids,
        pair_counts,
        area_table,
        fold_map,
    )
    return step_call(
        model_state, sea_mask, wave_speed, diffusivity, surface_gains, *exchanged
    )


def solution(mesh):
    in_specs = (
        P("comp", None, None, "tx", "ty"),
        P("comp", "tx", "ty"),
        P("comp", None),
        P("comp", None),
        P("comp", None),
        P(),
        P("comp", ("tx", "ty"), None, None),
        P("comp", ("tx", "ty"), None, None),
        P("comp", ("tx", "ty"), None, None),
        P("comp", ("tx", "ty"), None),
        P(),
    )
    out_specs = P("comp", None, None, "tx", "ty")
    return jax.shard_map(shards, mesh=mesh, in_specs=in_specs, out_specs=out_specs, check_vma=False)
```

```python
import jax
import jax.numpy as jnp
from jax import lax
from jax.experimental import pallas as pl
from jax.experimental.pallas import tpu as pltpu
from jax.sharding import PartitionSpec as P

MESH = pl.DeviceIdType.MESH
NEAR = 4
ROWS = 128
COLS = 256
f32 = jnp.float32
i32 = jnp.int32
f8 = jnp.float8_e4m3fn
dma = pltpu.SemaphoreType.DMA
GROUP = 8
PICK_UNROLL = 2
BATCH = 8


def exchange_kernel(
    counts,
    state,
    mask,
    own,
    target,
    ids,
    area,
    fold_map,
    places_out,
    weights_out,
    live_out,
    values_out,
    rows_out,
    columns_out,
    fields,
    sea,
    own_v,
    target_v,
    ids_v,
    area_v,
    fold_v,
    surface,
    early,
    late,
    rows_in,
    columns_in,
    arrived,
    places,
    weights,
    live,
    rows_got,
    columns_got,
    fold_got,
    load_sem,
    store_sem,
    early_send,
    early_recv,
    late_send,
    late_recv,
    edge_send,
    edge_recv,
    fold_send,
    fold_recv,
):
    levels = fields.shape[1]
    comps = lax.axis_size("comp")
    windows = comps - 1
    count_x = lax.axis_size("tx")
    count_y = lax.axis_size("ty")
    positions = count_x * count_y
    comp = lax.axis_index("comp")
    ix = lax.axis_index("tx")
    iy = lax.axis_index("ty")
    place = ix * count_y + iy
    is_ocean = comp == windows
    is_window = comp != windows
    on_fold = jnp.logical_and(is_ocean, iy == count_y - 1)
    offsets = [n % 2 + (n // 2) * count_y for n in range(NEAR)]

    def device_at(component, position):
        return (component, lax.div(position, count_y), lax.rem(position, count_y))

    loads = [
        pltpu.make_async_copy(target.at[0, 0], target_v, load_sem.at[0]),
        pltpu.make_async_copy(ids.at[0, 0], ids_v, load_sem.at[1]),
        pltpu.make_async_copy(own.at[0, 0], own_v, load_sem.at[2]),
        pltpu.make_async_copy(state.at[0, :, 0], fields.at[:, 0], load_sem.at[3]),
        pltpu.make_async_copy(
            state.at[0, :, pl.ds(1, levels - 1)], fields.at[:, pl.ds(1, levels - 1)], load_sem.at[4]
        ),
        pltpu.make_async_copy(mask.at[0], sea, load_sem.at[5]),
        pltpu.make_async_copy(area, area_v, load_sem.at[6]),
        pltpu.make_async_copy(fold_map.at[pl.ds(ix * ROWS, ROWS)], fold_v, load_sem.at[7]),
    ]
    for load in loads:
        load.start()

    west = (comp, lax.rem(ix + count_x - 1, count_x), iy)
    east = (comp, lax.rem(ix + 1, count_x), iy)
    south = (comp, ix, lax.rem(iy + count_y - 1, count_y))
    north = (comp, ix, lax.rem(iy + 1, count_y))

    barrier = pltpu.get_barrier_semaphore()
    for neighbour in (west, east, south, north):
        pl.semaphore_signal(barrier, inc=1, device_id=neighbour, device_id_type=MESH)
    sources = [lax.rem(place + positions - offset, positions) for offset in offsets]

    @pl.when(is_ocean)
    def _():
        for source in sources:
            for window in range(windows):
                pl.semaphore_signal(
                    barrier, inc=1, device_id=device_at(window, source), device_id_type=MESH
                )

    @pl.when(is_window)
    def _():
        for source in sources:
            pl.semaphore_signal(
                barrier, inc=1, device_id=device_at(windows, source), device_id_type=MESH
            )

    @pl.when(on_fold)
    def _():
        for step in range(1, count_x):
            pl.semaphore_signal(
                barrier,
                inc=1,
                device_id=(comp, lax.rem(ix + step, count_x), iy),
                device_id_type=MESH,
            )

    loads[0].wait()
    loads[1].wait()
    lane = lax.broadcasted_iota(jnp.int32, (1, COLS), 1)
    for n in range(NEAR):
        limit = counts[0, 0, n]
        for row in range(GROUP):
            span = slice(row * COLS, (row + 1) * COLS)
            cell = target_v[n : n + 1, span]
            early[n, row : row + 1] = jnp.where(lane + row * COLS < limit, cell, -1)
            early[n, GROUP + row : GROUP + row + 1] = ids_v[n : n + 1, span]

    slot = jnp.where(is_ocean, 0, comp * NEAR)

    def packet_copy(kind, n, window, component):
        position = lax.rem(place + offsets[n], positions)
        source, target_ref, send, recv = {
            "early": (early, arrived, early_send, early_recv),
            "late": (late, values_out, late_send, late_recv),
        }[kind]
        return pltpu.make_async_remote_copy(
            src_ref=source.at[n],
            dst_ref=target_ref.at[slot + n],
            send_sem=send.at[n * windows + window],
            recv_sem=recv.at[slot + n],
            device_id=device_at(component, position),
            device_id_type=MESH,
        )

    def send_packets(kind, n):
        @pl.when(is_ocean)
        def _():
            for window in range(windows):
                packet_copy(kind, n, window, window).start()

        @pl.when(is_window)
        def _():
            packet_copy(kind, n, 0, windows).start()

    loads[2].wait()
    loads[3].wait()
    for at, variable in enumerate((3, 1, 2)):
        turned = jnp.transpose(fields[variable, 0])
        high = turned.astype(jnp.bfloat16)
        low = (turned - high.astype(jnp.float32)).astype(jnp.bfloat16)
        surface[at * COLS : (at + 1) * COLS, 0:ROWS] = high
        surface[at * COLS : (at + 1) * COLS, ROWS : 2 * ROWS] = low

    row_ids = lax.broadcasted_iota(jnp.int32, (ROWS, COLS), 0)
    col_ids = lax.broadcasted_iota(jnp.int32, (COLS, COLS), 0)

    strip = ROWS // 2
    lanes = lax.broadcasted_iota(jnp.int32, (strip, 128), 1)

    def pack_strip(at, block):
        half = slice(at * 128, (at + 1) * 128)
        band = pl.ds(pl.multiple_of(block * strip, strip), strip)
        near, pair = (127, 126) if at else (0, 0)
        packed = jnp.where(
            lanes == 32,
            pltpu.roll(sea[band, half].astype(jnp.float32), (32 - near) % 128, 1),
            0.0,
        )
        for level in range(levels):
            turned = pltpu.roll(fields[0, level, band, half], (2 * level - pair) % 128, 1)
            packed = jnp.where((lanes >> 1) == level, turned, packed)
            for variable, first in ((2, 16), (3, 24)):
                turned = pltpu.roll(
                    fields[variable, level, band, half], (first + level - near) % 128, 1
                )
                packed = jnp.where(lanes == first + level, turned, packed)
        columns_in[at, band] = packed

    def pick(n, side):
        def pick_rows(part, carry):
            if side is not None:
                pack_strip(side, part)
            for step in range(GROUP // 2):
                row = part * (GROUP // 2) + step
                cell = own_v[n : n + 1, pl.ds(pl.multiple_of(row * COLS, COLS), COLS)]
                hot = jnp.where(row_ids == (cell >> 8), 1.0, 0.0).astype(jnp.bfloat16)
                chosen = jnp.dot(
                    surface[...],
                    jnp.concatenate([hot, hot], axis=0),
                    preferred_element_type=jnp.float32,
                )
                here = col_ids == (cell & (COLS - 1))
                for at in range(3):
                    part_of = jnp.where(here, chosen[at * COLS : (at + 1) * COLS], 0.0)
                    late[n, pl.ds(at * GROUP + row, 1), :] = jnp.sum(
                        part_of, axis=0, keepdims=True
                    )
            return carry

        lax.fori_loop(0, 2, pick_rows, 0, unroll=PICK_UNROLL)

    edge_copies = []
    for at, device in enumerate((west, east)):
        edge_copies.append(
            pltpu.make_async_remote_copy(
                src_ref=rows_in.at[at],
                dst_ref=rows_got.at[1 - at],
                send_sem=edge_send.at[at],
                recv_sem=edge_recv.at[1 - at],
                device_id=device,
                device_id_type=MESH,
            )
        )
    for at, device in enumerate((south, north)):
        edge_copies.append(
            pltpu.make_async_remote_copy(
                src_ref=columns_in.at[at],
                dst_ref=columns_got.at[1 - at],
                send_sem=edge_send.at[2 + at],
                recv_sem=edge_recv.at[2 + 1 - at],
                device_id=device,
                device_id_type=MESH,
            )
        )

    def fold_copy(step):
        return pltpu.make_async_remote_copy(
            src_ref=columns_in.at[1],
            dst_ref=fold_got.at[ix],
            send_sem=fold_send.at[step],
            recv_sem=fold_recv.at[step],
            device_id=(comp, lax.rem(ix + step, count_x), iy),
            device_id_type=MESH,
        )

    fold_keep = pltpu.make_async_copy(columns_in.at[1], fold_got.at[ix], fold_send.at[0])

    def send_edges():
        for at, (near, far) in enumerate(((0, 1), (ROWS - 1, ROWS - 2))):
            for level in range(levels):
                for item, (variable, row) in enumerate(((0, near), (0, far), (1, near), (3, near))):
                    rows_in[at, item * 8 + level : item * 8 + level + 1] = fields[
                        variable, level, row : row + 1, :
                    ]
            rows_in[at, 32:33] = sea[near : near + 1].astype(jnp.float32)
        for copy in edge_copies:
            copy.start()

        @pl.when(on_fold)
        def _():
            fold_keep.start()
            for step in range(1, count_x):
                fold_copy(step).start()

    pick(3, None)
    @pl.when(is_window)
    def _():
        pl.semaphore_wait(barrier, 4 + NEAR)

    @pl.when(jnp.logical_and(is_ocean, iy != count_y - 1))
    def _():
        pl.semaphore_wait(barrier, 4 + windows * NEAR)

    @pl.when(on_fold)
    def _():
        pl.semaphore_wait(barrier, 4 + windows * NEAR + count_x - 1)

    for n in reversed(range(NEAR)):
        send_packets("early", n)

    send_packets("late", 3)
    loads[4].wait()
    loads[5].wait()
    pick(2, 0)
    send_packets("late", 2)
    pick(1, 1)
    send_packets("late", 1)
    send_edges()
    pick(0, None)
    send_packets("late", 0)

    def wait_slot(kind, at):
        target_ref, recv, source = {
            "early": (arrived, early_recv, early),
            "late": (values_out, late_recv, late),
        }[kind]
        pltpu.make_async_remote_copy(
            src_ref=source.at[0],
            dst_ref=target_ref.at[at],
            send_sem=early_send.at[0],
            recv_sem=recv.at[at],
            device_id=west,
            device_id_type=MESH,
        ).wait_recv()

    def finish(kind):
        @pl.when(is_ocean)
        def _():
            for n in range(NEAR):
                for window in range(windows):
                    packet_copy(kind, n, window, window).wait_send()
            for at in range(windows * NEAR):
                wait_slot(kind, at)

        @pl.when(is_window)
        def _():
            for n in range(NEAR):
                packet_copy(kind, n, 0, windows).wait_send()
            for at in range(NEAR):
                wait_slot(kind, at)

    loads[6].wait()
    loads[7].wait()
    spare = windows * NEAR * GROUP
    places[0, spare : spare + GROUP] = jnp.zeros((GROUP, COLS), i32)
    places[1, spare : spare + GROUP] = jnp.full((GROUP, COLS), -1, i32)
    table = [
        jnp.broadcast_to(area_v[at * 128 : (at + 1) * 128][None], (GROUP, 128)) for at in range(2)
    ]
    slot_ids = lax.broadcasted_iota(
        jnp.int32, (GROUP, COLS), 0
    ) * COLS + lax.broadcasted_iota(jnp.int32, (GROUP, COLS), 1)
    mine = jnp.logical_or(slot_ids - 3 * ((slot_ids * 43691) >> 17) == comp, is_ocean)
    finish("early")

    def place_packets(group, carry):
        for n in range(NEAR):
            at = group * NEAR + n
            cell = arrived[at, 0:GROUP]
            entry = arrived[at, GROUP : 2 * GROUP]
            lines = pl.ds(pl.multiple_of(at * GROUP, GROUP), GROUP)
            for half in range(2):
                span = slice(half * 128, (half + 1) * 128)
                index = entry[:, span]
                low = jnp.take_along_axis(table[0], index & 127, axis=1, mode="promise_in_bounds")
                high = jnp.take_along_axis(table[1], index & 127, axis=1, mode="promise_in_bounds")
                weights[lines, span] = jnp.where(index < 128, low, high)
            row = cell >> 8
            places[0, lines] = row & 63
            alive = jnp.logical_and(cell >= 0, mine)
            places[1, lines] = jnp.where(alive, ((row >> 6) << 8) + (cell & (COLS - 1)), -1)
            used = jnp.sum(jnp.where(cell >= 0, 1.0, 0.0), axis=0, keepdims=True)
            used = jnp.sum(used, axis=1, keepdims=True)
            live[pl.ds(at, 1)] = jnp.broadcast_to(used, (1, 128)).astype(jnp.int32)
        return carry

    lax.fori_loop(0, jnp.where(is_ocean, windows, 1), place_packets, 0)
    stores = [
        pltpu.make_async_copy(places, places_out, store_sem.at[0]),
        pltpu.make_async_copy(weights, weights_out, store_sem.at[1]),
        pltpu.make_async_copy(live, live_out, store_sem.at[2]),
        pltpu.make_async_copy(rows_got, rows_out, store_sem.at[3]),
        pltpu.make_async_copy(columns_got, columns_out, store_sem.at[4]),
    ]
    for store in stores[:3]:
        store.start()

    for copy in edge_copies:
        copy.wait_send()
        copy.wait_recv()
    one = jnp.float32(1.0)
    zero = jnp.float32(0.0)
    rows_got[0] = rows_got[0] * jnp.where(jnp.logical_or(is_ocean, ix > 0), one, zero)
    rows_got[1] = rows_got[1] * jnp.where(jnp.logical_or(is_ocean, ix < count_x - 1), one, zero)
    columns_got[0] = columns_got[0] * jnp.where(iy > 0, one, zero)
    columns_got[1] = columns_got[1] * jnp.where(iy < count_y - 1, one, zero)

    @pl.when(on_fold)
    def _():
        fold_keep.wait()
        for step in range(1, count_x):
            fold_copy(step).wait_send()
            fold_copy(step).wait_recv()
        wanted = jnp.transpose(jnp.broadcast_to(fold_v[...][None], (ROWS, ROWS)))
        lanes = lax.broadcasted_iota(jnp.int32, (ROWS, 128), 1)
        gathered = jnp.zeros((ROWS, 128), f32)
        for block in range(count_x):
            hot = jnp.where(wanted == lanes + block * ROWS, 1.0, 0.0).astype(jnp.bfloat16)
            rest = fold_got[block]
            for part in range(3):
                piece = rest.astype(jnp.bfloat16)
                rest = rest - piece.astype(f32)
                gathered += jnp.dot(hot, piece, preferred_element_type=f32)
        swapped = jnp.where(
            (lanes & 1) == 0, pltpu.roll(gathered, 127, 1), pltpu.roll(gathered, 1, 1)
        )
        gathered = jnp.where(lanes < 16, swapped, gathered)
        turned = jnp.logical_and(lanes >= 16, lanes < 24)
        columns_got[1] = jnp.where(turned, -gathered, gathered)

    for store in stores[3:]:
        store.start()
    finish("late")
    for store in stores:
        store.wait()


def step_kernel(
    wave,
    spread,
    gains,
    state,
    mask,
    places,
    weights,
    live,
    values,
    rows,
    columns,
    result,
    fields,
    updated,
    land,
    places_v,
    weights_v,
    values_v,
    rows_v,
    columns_v,
    sea_v,
    addends,
    live_s,
    order,
    left,
    right,
    total,
    load_sem,
    level_sem,
    store_sem,
):
    levels = fields.shape[0]
    windows = lax.axis_size("comp") - 1
    count_x = lax.axis_size("tx")
    count_y = lax.axis_size("ty")
    comp = lax.axis_index("comp")
    ix = lax.axis_index("tx")
    iy = lax.axis_index("ty")
    is_ocean = comp == windows
    packets = values_v.shape[0]

    def level_load(level):
        return pltpu.make_async_copy(state.at[0, :, level], fields.at[level], level_sem.at[level])

    def level_store(level):
        return pltpu.make_async_copy(
            updated.at[level], result.at[0, :, level], store_sem.at[level]
        )

    loads = [
        pltpu.make_async_copy(live, live_s, load_sem.at[0]),
        pltpu.make_async_copy(values, values_v, load_sem.at[1]),
        pltpu.make_async_copy(weights, weights_v, load_sem.at[2]),
        pltpu.make_async_copy(places, places_v, load_sem.at[3]),
        pltpu.make_async_copy(mask.at[0], sea_v, load_sem.at[4]),
        pltpu.make_async_copy(rows, rows_v, load_sem.at[5]),
        pltpu.make_async_copy(columns, columns_v, load_sem.at[6]),
    ]
    for load in loads:
        load.start()
    for level in range(levels):
        level_load(level).start()

    spare = packets * GROUP
    addends[:, spare : spare + GROUP] = jnp.zeros((12, GROUP, COLS), f32)
    total[...] = jnp.zeros_like(total)
    for at in range(spare + GROUP):
        order[at] = spare
    loads[0].wait()

    def list_packet(at, count):
        lines = (live_s[at, 0] + COLS - 1) // COLS

        def list_row(row, carry):
            order[count + row] = at * GROUP + row
            return carry

        lax.fori_loop(0, lines, list_row, 0)
        return count + lines

    live_lines = lax.fori_loop(0, jnp.where(is_ocean, packets, NEAR), list_packet, 0)

    for load in loads[1:]:
        load.wait()

    def split_packets(group, carry):
        for n in range(NEAR):
            at = group * NEAR + n
            lines = pl.ds(pl.multiple_of(at * GROUP, GROUP), GROUP)
            weight = weights_v[lines] * 64.0
            for item in range(4):
                value = weight
                if item < 3:
                    value = weight * values_v[at, item * GROUP : (item + 1) * GROUP]
                for part in range(3):
                    piece = value.astype(f8).astype(f32)
                    addends[part * 4 + item, lines] = piece
                    value = (value - piece) * 16.0
        return carry

    lax.fori_loop(0, jnp.where(is_ocean, packets // NEAR, 1), split_packets, 0)
    land[...] = 1.0 - sea_v[...].astype(jnp.float32)
    one = jnp.float32(1.0)
    zero = jnp.float32(0.0)
    valid_west = jnp.where(jnp.logical_or(is_ocean, ix > 0), one, zero)
    valid_east = jnp.where(jnp.logical_or(is_ocean, ix < count_x - 1), one, zero)
    valid_south = jnp.where(iy > 0, one, zero)
    valid_north = jnp.where(jnp.logical_or(is_ocean, iy < count_y - 1), one, zero)

    row_ids = lax.broadcasted_iota(jnp.int32, (ROWS, COLS), 0)
    col_ids = lax.broadcasted_iota(jnp.int32, (ROWS, COLS), 1)
    is_first_row = row_ids == 0
    is_last_row = row_ids == ROWS - 1
    is_first_col = col_ids == 0
    is_last_col = col_ids == COLS - 1
    ocean_share = jnp.where(is_ocean, one, zero)

    def before_x(field, edge):
        return jnp.where(is_first_row, edge, pltpu.roll(field, 1, 0))

    def after_x(field, edge):
        return jnp.where(is_last_row, edge, pltpu.roll(field, ROWS - 1, 0))

    def before_y(field, edge):
        return jnp.where(is_first_col, edge, pltpu.roll(field, 1, 1))

    def after_y(field, edge):
        return jnp.where(is_last_col, edge, pltpu.roll(field, COLS - 1, 1))

    def stencil(level):
        level_load(level).wait()
        pressure = fields[level, 0]
        zonal = fields[level, 1]
        meridional = fields[level, 2]
        tracer = fields[level, 3]
        half_wave = 0.5 * wave[0, level]
        drag = jnp.where(is_ocean, one, jnp.where(level == 0, gains[0, 2], zero))
        keeping = 1.0 - drag * land[...]
        tendency = 1.0 - ocean_share * land[...]
        edge_rows = [
            [rows_v[side, pl.ds(item * 8 + level, 1), :] for item in range(4)] for side in range(2)
        ]
        edge_cols = []
        for side in range(2):
            pairs = pltpu.roll(columns_v[side], lax.rem(128 - 2 * level, 128), 1)
            others = pltpu.roll(columns_v[side], lax.rem(128 - level, 128), 1)
            edge_cols.append(
                [
                    pairs[:, 1 - side : 2 - side],
                    pairs[:, side : side + 1],
                    others[:, 16:17],
                    others[:, 24:25],
                ]
            )
        row_keep = [
            (1.0 - drag * (1.0 - rows_v[0, 32:33, :])) * valid_west,
            (1.0 - drag * (1.0 - rows_v[1, 32:33, :])) * valid_east,
        ]
        col_keep = [
            (1.0 - drag * (1.0 - columns_v[0, :, 32:33])) * valid_south,
            (1.0 - drag * (1.0 - columns_v[1, :, 32:33])) * valid_north,
        ]
        new_zonal = keeping * (
            zonal
            - half_wave
            * (after_x(pressure, edge_rows[1][0]) - before_x(pressure, edge_rows[0][0]))
        )
        new_meridional = keeping * (
            meridional
            - half_wave
            * (after_y(pressure, edge_cols[1][0]) - before_y(pressure, edge_cols[0][0]))
        )
        zonal_west = row_keep[0] * (
            edge_rows[0][2] - half_wave * (pressure[0:1] - edge_rows[0][1])
        )
        zonal_east = row_keep[1] * (
            edge_rows[1][2] - half_wave * (edge_rows[1][1] - pressure[ROWS - 1 : ROWS])
        )
        meridional_south = col_keep[0] * (
            edge_cols[0][2] - half_wave * (pressure[:, 0:1] - edge_cols[0][1])
        )
        meridional_north = col_keep[1] * (
            edge_cols[1][2] - half_wave * (edge_cols[1][1] - pressure[:, COLS - 1 : COLS])
        )
        divergence = (
            after_x(new_zonal, zonal_east)
            - before_x(new_zonal, zonal_west)
            + after_y(new_meridional, meridional_north)
            - before_y(new_meridional, meridional_south)
        )
        laplace = (
            after_x(tracer, edge_rows[1][3])
            + before_x(tracer, edge_rows[0][3])
            + after_y(tracer, edge_cols[1][3])
            + before_y(tracer, edge_cols[0][3])
            - 4.0 * tracer
        )
        updated[level, 0] = pressure - half_wave * divergence
        updated[level, 1] = new_zonal
        updated[level, 2] = new_meridional
        updated[level, 3] = tracer + spread[0, level] * tendency * laplace

    narrow_ids = lax.broadcasted_iota(jnp.int16, (64, COLS), 0)
    wide_ids = lax.broadcasted_iota(jnp.int16, (2 * COLS, COLS), 0)
    one16 = jnp.ones((), jnp.bfloat16)
    zero16 = jnp.zeros((), jnp.bfloat16)

    def repeated(line, count, kind):
        tile = jnp.broadcast_to(line, (16, COLS)).astype(kind)
        return jnp.concatenate([tile] * (count // 16), axis=0)

    def scatter(batch):
        for at in range(BATCH):
            line = pl.ds(order[batch * BATCH + at], 1)
            span = slice(at * COLS, (at + 1) * COLS)
            here = narrow_ids == repeated(places_v[0, line, :], 64, jnp.int16)
            for item in range(4):
                for part in range(3):
                    value = addends[part * 4 + item, line, :]
                    lead = (part * 4 + item) * 64
                    left[lead : lead + 64, span] = jnp.where(
                        here, repeated(value, 64, jnp.bfloat16), zero16
                    ).astype(f8)
            there = wide_ids == repeated(places_v[1, line, :], 2 * COLS, jnp.int16)
            right[:, span] = jnp.where(there, one16, zero16).astype(f8)
        total[...] += lax.dot_general(
            left[...],
            right[...],
            (((1,), (1,)), ((), ())),
            preferred_element_type=jnp.float32,
        )

    def level_step(level, carry):
        stencil(level)
        scatter(level)

        @pl.when(level > 0)
        def _():
            level_store(level).start()

        return carry

    lax.fori_loop(0, levels, level_step, 0)

    def extra_step(batch, carry):
        scatter(batch)
        return carry

    lax.fori_loop(levels, jnp.maximum(levels, (live_lines + BATCH - 1) // BATCH), extra_step, 0)

    for half in range(2):
        span = slice(half * 64, (half + 1) * 64)
        lanes = slice(half * COLS, (half + 1) * COLS)
        sums = [
            total[item * 64 : (item + 1) * 64, lanes] * (1.0 / 64.0)
            + total[256 + item * 64 : 256 + (item + 1) * 64, lanes] * (1.0 / 1024.0)
            + total[512 + item * 64 : 512 + (item + 1) * 64, lanes] * (1.0 / 16384.0)
            for item in range(4)
        ]
        tendency = 1.0 - ocean_share * land[span]
        for item, variable in enumerate((3, 1, 2)):
            gain = gains[0, 0] if variable == 3 else gains[0, 1]
            updated[0, variable, span] = updated[0, variable, span] + tendency * gain * (
                sums[item] - sums[3] * fields[0, variable, span]
            )
    level_store(0).start()
    for level in range(levels):
        level_store(level).wait()


def exchange_call(
    model_state, sea_mask, own_cells, target_cells, weight_ids, pair_counts, area_table, fold_map
):
    levels = model_state.shape[2]
    packets = (lax.axis_size("comp") - 1) * NEAR
    lines = packets * GROUP
    count_x = lax.axis_size("tx")
    anywhere = pl.BlockSpec(memory_space=pl.ANY)
    shapes = [
        ((2, lines + GROUP, COLS), i32),
        ((lines, COLS), f32),
        ((16, 128), i32),
        ((packets, 3 * GROUP, COLS), f32),
        ((2, 40, COLS), f32),
        ((2, ROWS, 128), f32),
    ]
    return pl.pallas_call(
        exchange_kernel,
        out_shape=tuple(jax.ShapeDtypeStruct(shape, kind) for shape, kind in shapes),
        in_specs=[pl.BlockSpec(memory_space=pltpu.SMEM)] + [anywhere] * 7,
        out_specs=[anywhere] * 6,
        scratch_shapes=[
            pltpu.VMEM((4, levels, ROWS, COLS), f32),
            pltpu.VMEM((ROWS, COLS), i32),
            pltpu.VMEM((NEAR, GROUP * COLS), i32),
            pltpu.VMEM((NEAR, GROUP * COLS), i32),
            pltpu.VMEM((NEAR, GROUP * COLS), i32),
            pltpu.VMEM(area_table.shape, f32),
            pltpu.VMEM((ROWS,), i32),
            pltpu.VMEM((3 * COLS, 2 * ROWS), jnp.bfloat16),
            pltpu.VMEM((NEAR, 2 * GROUP, COLS), i32),
            pltpu.VMEM((NEAR, 3 * GROUP, COLS), f32),
            pltpu.VMEM((2, 40, COLS), f32),
            pltpu.VMEM((2, ROWS, 128), f32),
            pltpu.VMEM((packets, 2 * GROUP, COLS), i32),
            pltpu.VMEM((2, lines + GROUP, COLS), i32),
            pltpu.VMEM((lines, COLS), f32),
            pltpu.VMEM((16, 128), i32),
            pltpu.VMEM((2, 40, COLS), f32),
            pltpu.VMEM((2, ROWS, 128), f32),
            pltpu.VMEM((count_x, ROWS, 128), f32),
            dma((8,)),
            dma((5,)),
            dma((packets,)),
            dma((packets,)),
            dma((packets,)),
            dma((packets,)),
            dma((4,)),
            dma((4,)),
            dma((count_x,)),
            dma((count_x,)),
        ],
        compiler_params=pltpu.CompilerParams(
            collective_id=0, has_side_effects=True, vmem_limit_bytes=60 * 2**20
        ),
        name="exchange",
    )(
        pair_counts,
        model_state,
        sea_mask,
        own_cells,
        target_cells,
        weight_ids,
        area_table,
        fold_map,
    )


def step_call(
    model_state,
    sea_mask,
    wave_speed,
    diffusivity,
    surface_gains,
    places,
    weights,
    live,
    values,
    rows,
    columns,
):
    levels = model_state.shape[2]
    lines = places.shape[1]
    anywhere = pl.BlockSpec(memory_space=pl.ANY)
    scalars = pl.BlockSpec(memory_space=pltpu.SMEM)
    return pl.pallas_call(
        step_kernel,
        out_shape=jax.ShapeDtypeStruct(model_state.shape, f32),
        in_specs=[scalars] * 3 + [anywhere] * 8,
        out_specs=anywhere,
        scratch_shapes=[
            pltpu.VMEM((levels, 4, ROWS, COLS), f32),
            pltpu.VMEM((levels, 4, ROWS, COLS), f32),
            pltpu.VMEM((ROWS, COLS), f32),
            pltpu.VMEM(places.shape, i32),
            pltpu.VMEM(weights.shape, f32),
            pltpu.VMEM(values.shape, f32),
            pltpu.VMEM(rows.shape, f32),
            pltpu.VMEM(columns.shape, f32),
            pltpu.VMEM((ROWS, COLS), i32),
            pltpu.VMEM((12, lines, COLS), f32),
            pltpu.SMEM(live.shape, i32),
            pltpu.SMEM((lines,), i32),
            pltpu.VMEM((3 * 4 * 64, BATCH * COLS), f8),
            pltpu.VMEM((2 * COLS, BATCH * COLS), f8),
            pltpu.VMEM((3 * 4 * 64, 2 * COLS), f32),
            dma((7,)),
            dma((levels,)),
            dma((levels,)),
        ],
        compiler_params=pltpu.CompilerParams(vmem_limit_bytes=60 * 2**20),
        name="step",
    )(
        wave_speed,
        diffusivity,
        surface_gains,
        model_state,
        sea_mask,
        places,
        weights,
        live,
        values,
        rows,
        columns,
    )


def shards(
    model_state,
    sea_mask,
    wave_speed,
    diffusivity,
    surface_gains,
    area_table,
    own_cells,
    target_cells,
    weight_ids,
    pair_counts,
    fold_map,
):
    exchanged = exchange_call(
        model_state,
        sea_mask,
        own_cells,
        target_cells,
        weight_ids,
        pair_counts,
        area_table,
        fold_map,
    )
    return step_call(
        model_state, sea_mask, wave_speed, diffusivity, surface_gains, *exchanged
    )


def solution(mesh):
    in_specs = (
        P("comp", None, None, "tx", "ty"),
        P("comp", "tx", "ty"),
        P("comp", None),
        P("comp", None),
        P("comp", None),
        P(),
        P("comp", ("tx", "ty"), None, None),
        P("comp", ("tx", "ty"), None, None),
        P("comp", ("tx", "ty"), None, None),
        P("comp", ("tx", "ty"), None),
        P(),
    )
    out_specs = P("comp", None, None, "tx", "ty")
    return jax.shard_map(shards, mesh=mesh, in_specs=in_specs, out_specs=out_specs, check_vma=False)
```

```python
import jax
import jax.numpy as jnp
from jax import lax
from jax.experimental import pallas as pl
from jax.experimental.pallas import tpu as pltpu
from jax.sharding import PartitionSpec as P

MESH = pl.DeviceIdType.MESH
NEAR = 4
ROWS = 128
COLS = 256
f32 = jnp.float32
i32 = jnp.int32
f8 = jnp.float8_e4m3fn
dma = pltpu.SemaphoreType.DMA
GROUP = 8
PICK_UNROLL = 2
BATCH = 8


def exchange_kernel(
    counts,
    state,
    mask,
    own,
    target,
    ids,
    area,
    fold_map,
    places_out,
    weights_out,
    live_out,
    values_out,
    rows_out,
    columns_out,
    fields,
    sea,
    own_v,
    target_v,
    ids_v,
    area_v,
    fold_v,
    surface,
    early,
    late,
    rows_in,
    columns_in,
    arrived,
    places,
    weights,
    live,
    rows_got,
    columns_got,
    fold_got,
    load_sem,
    store_sem,
    early_send,
    early_recv,
    late_send,
    late_recv,
    edge_send,
    edge_recv,
    fold_send,
    fold_recv,
):
    levels = fields.shape[1]
    comps = lax.axis_size("comp")
    windows = comps - 1
    count_x = lax.axis_size("tx")
    count_y = lax.axis_size("ty")
    positions = count_x * count_y
    comp = lax.axis_index("comp")
    ix = lax.axis_index("tx")
    iy = lax.axis_index("ty")
    place = ix * count_y + iy
    is_ocean = comp == windows
    is_window = comp != windows
    on_fold = jnp.logical_and(is_ocean, iy == count_y - 1)
    offsets = [n % 2 + (n // 2) * count_y for n in range(NEAR)]

    def device_at(component, position):
        return (component, lax.div(position, count_y), lax.rem(position, count_y))

    loads = [
        pltpu.make_async_copy(target.at[0, 0], target_v, load_sem.at[0]),
        pltpu.make_async_copy(ids.at[0, 0], ids_v, load_sem.at[1]),
        pltpu.make_async_copy(own.at[0, 0], own_v, load_sem.at[2]),
        pltpu.make_async_copy(state.at[0, :, 0], fields.at[:, 0], load_sem.at[3]),
        pltpu.make_async_copy(
            state.at[0, :, pl.ds(1, levels - 1)], fields.at[:, pl.ds(1, levels - 1)], load_sem.at[4]
        ),
        pltpu.make_async_copy(mask.at[0], sea, load_sem.at[5]),
        pltpu.make_async_copy(area, area_v, load_sem.at[6]),
        pltpu.make_async_copy(fold_map.at[pl.ds(ix * ROWS, ROWS)], fold_v, load_sem.at[7]),
    ]
    for load in loads:
        load.start()

    west = (comp, lax.rem(ix + count_x - 1, count_x), iy)
    east = (comp, lax.rem(ix + 1, count_x), iy)
    south = (comp, ix, lax.rem(iy + count_y - 1, count_y))
    north = (comp, ix, lax.rem(iy + 1, count_y))

    barrier = pltpu.get_barrier_semaphore()
    for neighbour in (west, east, south, north):
        pl.semaphore_signal(barrier, inc=1, device_id=neighbour, device_id_type=MESH)
    sources = [lax.rem(place + positions - offset, positions) for offset in offsets]

    @pl.when(is_ocean)
    def _():
        for source in sources:
            for window in range(windows):
                pl.semaphore_signal(
                    barrier, inc=1, device_id=device_at(window, source), device_id_type=MESH
                )

    @pl.when(is_window)
    def _():
        for source in sources:
            pl.semaphore_signal(
                barrier, inc=1, device_id=device_at(windows, source), device_id_type=MESH
            )

    @pl.when(on_fold)
    def _():
        for step in range(1, count_x):
            pl.semaphore_signal(
                barrier,
                inc=1,
                device_id=(comp, lax.rem(ix + step, count_x), iy),
                device_id_type=MESH,
            )

    loads[0].wait()
    loads[1].wait()
    lane = lax.broadcasted_iota(jnp.int32, (1, COLS), 1)
    for n in range(NEAR):
        limit = counts[0, 0, n]
        for row in range(GROUP):
            span = slice(row * COLS, (row + 1) * COLS)
            cell = target_v[n : n + 1, span]
            early[n, row : row + 1] = jnp.where(lane + row * COLS < limit, cell, -1)
            early[n, GROUP + row : GROUP + row + 1] = ids_v[n : n + 1, span]

    slot = jnp.where(is_ocean, 0, comp * NEAR)

    def packet_copy(kind, n, window, component):
        position = lax.rem(place + offsets[n], positions)
        source, target_ref, send, recv = {
            "early": (early, arrived, early_send, early_recv),
            "late": (late, values_out, late_send, late_recv),
        }[kind]
        return pltpu.make_async_remote_copy(
            src_ref=source.at[n],
            dst_ref=target_ref.at[slot + n],
            send_sem=send.at[n * windows + window],
            recv_sem=recv.at[slot + n],
            device_id=device_at(component, position),
            device_id_type=MESH,
        )

    def send_packets(kind, n):
        @pl.when(is_ocean)
        def _():
            for window in range(windows):
                packet_copy(kind, n, window, window).start()

        @pl.when(is_window)
        def _():
            packet_copy(kind, n, 0, windows).start()

    loads[2].wait()
    loads[3].wait()
    for at, variable in enumerate((3, 1, 2)):
        turned = jnp.transpose(fields[variable, 0])
        high = turned.astype(jnp.bfloat16)
        low = (turned - high.astype(jnp.float32)).astype(jnp.bfloat16)
        surface[at * COLS : (at + 1) * COLS, 0:ROWS] = high
        surface[at * COLS : (at + 1) * COLS, ROWS : 2 * ROWS] = low

    row_ids = lax.broadcasted_iota(jnp.int32, (ROWS, COLS), 0)
    col_ids = lax.broadcasted_iota(jnp.int32, (COLS, COLS), 0)

    strip = ROWS // 2
    lanes = lax.broadcasted_iota(jnp.int32, (strip, 128), 1)

    def pack_strip(at, block):
        half = slice(at * 128, (at + 1) * 128)
        band = pl.ds(pl.multiple_of(block * strip, strip), strip)
        near, pair = (127, 126) if at else (0, 0)
        packed = jnp.where(
            lanes == 32,
            pltpu.roll(sea[band, half].astype(jnp.float32), (32 - near) % 128, 1),
            0.0,
        )
        for level in range(levels):
            turned = pltpu.roll(fields[0, level, band, half], (2 * level - pair) % 128, 1)
            packed = jnp.where((lanes >> 1) == level, turned, packed)
            for variable, first in ((2, 16), (3, 24)):
                turned = pltpu.roll(
                    fields[variable, level, band, half], (first + level - near) % 128, 1
                )
                packed = jnp.where(lanes == first + level, turned, packed)
        columns_in[at, band] = packed

    def pick(n, side):
        def pick_rows(part, carry):
            if side is not None:
                pack_strip(side, part)
            for step in range(GROUP // 2):
                row = part * (GROUP // 2) + step
                cell = own_v[n : n + 1, pl.ds(pl.multiple_of(row * COLS, COLS), COLS)]
                hot = jnp.where(row_ids == (cell >> 8), 1.0, 0.0).astype(jnp.bfloat16)
                chosen = jnp.dot(
                    surface[...],
                    jnp.concatenate([hot, hot], axis=0),
                    preferred_element_type=jnp.float32,
                )
                here = col_ids == (cell & (COLS - 1))
                for at in range(3):
                    part_of = jnp.where(here, chosen[at * COLS : (at + 1) * COLS], 0.0)
                    late[n, pl.ds(at * GROUP + row, 1), :] = jnp.sum(
                        part_of, axis=0, keepdims=True
                    )
            return carry

        lax.fori_loop(0, 2, pick_rows, 0, unroll=PICK_UNROLL)

    edge_copies = []
    for at, device in enumerate((west, east)):
        edge_copies.append(
            pltpu.make_async_remote_copy(
                src_ref=rows_in.at[at],
                dst_ref=rows_got.at[1 - at],
                send_sem=edge_send.at[at],
                recv_sem=edge_recv.at[1 - at],
                device_id=device,
                device_id_type=MESH,
            )
        )
    for at, device in enumerate((south, north)):
        edge_copies.append(
            pltpu.make_async_remote_copy(
                src_ref=columns_in.at[at],
                dst_ref=columns_got.at[1 - at],
                send_sem=edge_send.at[2 + at],
                recv_sem=edge_recv.at[2 + 1 - at],
                device_id=device,
                device_id_type=MESH,
            )
        )

    def fold_copy(step):
        return pltpu.make_async_remote_copy(
            src_ref=columns_in.at[1],
            dst_ref=fold_got.at[ix],
            send_sem=fold_send.at[step],
            recv_sem=fold_recv.at[step],
            device_id=(comp, lax.rem(ix + step, count_x), iy),
            device_id_type=MESH,
        )

    fold_keep = pltpu.make_async_copy(columns_in.at[1], fold_got.at[ix], fold_send.at[0])

    def send_edges():
        for at, (near, far) in enumerate(((0, 1), (ROWS - 1, ROWS - 2))):
            for level in range(levels):
                for item, (variable, row) in enumerate(((0, near), (0, far), (1, near), (3, near))):
                    rows_in[at, item * 8 + level : item * 8 + level + 1] = fields[
                        variable, level, row : row + 1, :
                    ]
            rows_in[at, 32:33] = sea[near : near + 1].astype(jnp.float32)
        for copy in edge_copies:
            copy.start()

        @pl.when(on_fold)
        def _():
            fold_keep.start()
            for step in range(1, count_x):
                fold_copy(step).start()

    pick(3, None)
    @pl.when(is_window)
    def _():
        pl.semaphore_wait(barrier, 4 + NEAR)

    @pl.when(jnp.logical_and(is_ocean, iy != count_y - 1))
    def _():
        pl.semaphore_wait(barrier, 4 + windows * NEAR)

    @pl.when(on_fold)
    def _():
        pl.semaphore_wait(barrier, 4 + windows * NEAR + count_x - 1)

    for n in reversed(range(NEAR)):
        send_packets("early", n)

    send_packets("late", 3)
    loads[4].wait()
    loads[5].wait()
    pick(2, 0)
    send_packets("late", 2)
    pick(1, 1)
    send_packets("late", 1)
    send_edges()
    pick(0, None)
    send_packets("late", 0)

    def wait_slot(kind, at):
        target_ref, recv, source = {
            "early": (arrived, early_recv, early),
            "late": (values_out, late_recv, late),
        }[kind]
        pltpu.make_async_remote_copy(
            src_ref=source.at[0],
            dst_ref=target_ref.at[at],
            send_sem=early_send.at[0],
            recv_sem=recv.at[at],
            device_id=west,
            device_id_type=MESH,
        ).wait_recv()

    def finish(kind):
        @pl.when(is_ocean)
        def _():
            for n in range(NEAR):
                for window in range(windows):
                    packet_copy(kind, n, window, window).wait_send()
            for at in range(windows * NEAR):
                wait_slot(kind, at)

        @pl.when(is_window)
        def _():
            for n in range(NEAR):
                packet_copy(kind, n, 0, windows).wait_send()
            for at in range(NEAR):
                wait_slot(kind, at)

    loads[6].wait()
    loads[7].wait()
    spare = windows * NEAR * GROUP
    places[0, spare : spare + GROUP] = jnp.zeros((GROUP, COLS), i32)
    places[1, spare : spare + GROUP] = jnp.full((GROUP, COLS), -1, i32)
    table = [
        jnp.broadcast_to(area_v[at * 128 : (at + 1) * 128][None], (GROUP, 128)) for at in range(2)
    ]
    slot_ids = lax.broadcasted_iota(
        jnp.int32, (GROUP, COLS), 0
    ) * COLS + lax.broadcasted_iota(jnp.int32, (GROUP, COLS), 1)
    mine = jnp.logical_or(slot_ids - 3 * ((slot_ids * 43691) >> 17) == comp, is_ocean)
    finish("early")

    def place_packets(group, carry):
        for n in range(NEAR):
            at = group * NEAR + n
            cell = arrived[at, 0:GROUP]
            entry = arrived[at, GROUP : 2 * GROUP]
            lines = pl.ds(pl.multiple_of(at * GROUP, GROUP), GROUP)
            for half in range(2):
                span = slice(half * 128, (half + 1) * 128)
                index = entry[:, span]
                low = jnp.take_along_axis(table[0], index & 127, axis=1, mode="promise_in_bounds")
                high = jnp.take_along_axis(table[1], index & 127, axis=1, mode="promise_in_bounds")
                weights[lines, span] = jnp.where(index < 128, low, high)
            row = cell >> 8
            places[0, lines] = row & 63
            alive = jnp.logical_and(cell >= 0, mine)
            places[1, lines] = jnp.where(alive, ((row >> 6) << 8) + (cell & (COLS - 1)), -1)
            used = jnp.sum(jnp.where(cell >= 0, 1.0, 0.0), axis=0, keepdims=True)
            used = jnp.sum(used, axis=1, keepdims=True)
            live[pl.ds(at, 1)] = jnp.broadcast_to(used, (1, 128)).astype(jnp.int32)
        return carry

    lax.fori_loop(0, jnp.where(is_ocean, windows, 1), place_packets, 0)
    stores = [
        pltpu.make_async_copy(places, places_out, store_sem.at[0]),
        pltpu.make_async_copy(weights, weights_out, store_sem.at[1]),
        pltpu.make_async_copy(live, live_out, store_sem.at[2]),
        pltpu.make_async_copy(rows_got, rows_out, store_sem.at[3]),
        pltpu.make_async_copy(columns_got, columns_out, store_sem.at[4]),
    ]
    for store in stores[:3]:
        store.start()

    for copy in edge_copies:
        copy.wait_send()
        copy.wait_recv()
    one = jnp.float32(1.0)
    zero = jnp.float32(0.0)
    rows_got[0] = rows_got[0] * jnp.where(jnp.logical_or(is_ocean, ix > 0), one, zero)
    rows_got[1] = rows_got[1] * jnp.where(jnp.logical_or(is_ocean, ix < count_x - 1), one, zero)
    columns_got[0] = columns_got[0] * jnp.where(iy > 0, one, zero)
    columns_got[1] = columns_got[1] * jnp.where(iy < count_y - 1, one, zero)

    @pl.when(on_fold)
    def _():
        fold_keep.wait()
        for step in range(1, count_x):
            fold_copy(step).wait_send()
            fold_copy(step).wait_recv()
        wanted = jnp.transpose(jnp.broadcast_to(fold_v[...][None], (ROWS, ROWS)))
        lanes = lax.broadcasted_iota(jnp.int32, (ROWS, 128), 1)
        gathered = jnp.zeros((ROWS, 128), f32)
        for block in range(count_x):
            hot = jnp.where(wanted == lanes + block * ROWS, 1.0, 0.0).astype(jnp.bfloat16)
            rest = fold_got[block]
            for part in range(3):
                piece = rest.astype(jnp.bfloat16)
                rest = rest - piece.astype(f32)
                gathered += jnp.dot(hot, piece, preferred_element_type=f32)
        swapped = jnp.where(
            (lanes & 1) == 0, pltpu.roll(gathered, 127, 1), pltpu.roll(gathered, 1, 1)
        )
        gathered = jnp.where(lanes < 16, swapped, gathered)
        turned = jnp.logical_and(lanes >= 16, lanes < 24)
        columns_got[1] = jnp.where(turned, -gathered, gathered)

    for store in stores[3:]:
        store.start()
    finish("late")
    for store in stores:
        store.wait()


def step_kernel(
    wave,
    spread,
    gains,
    state,
    mask,
    places,
    weights,
    live,
    values,
    rows,
    columns,
    result,
    fields,
    updated,
    land,
    places_v,
    weights_v,
    values_v,
    rows_v,
    columns_v,
    sea_v,
    addends,
    live_s,
    order,
    left,
    right,
    total,
    load_sem,
    level_sem,
    store_sem,
):
    levels = fields.shape[0]
    windows = lax.axis_size("comp") - 1
    count_x = lax.axis_size("tx")
    count_y = lax.axis_size("ty")
    comp = lax.axis_index("comp")
    ix = lax.axis_index("tx")
    iy = lax.axis_index("ty")
    is_ocean = comp == windows
    packets = values_v.shape[0]

    def level_load(level):
        return pltpu.make_async_copy(state.at[0, :, level], fields.at[level], level_sem.at[level])

    def first_store(half):
        span = pl.ds(half * 64, 64)
        return pltpu.make_async_copy(
            updated.at[0, :, span], result.at[0, :, 0, span], store_sem.at[half * levels]
        )

    def level_store(level):
        return pltpu.make_async_copy(
            updated.at[level], result.at[0, :, level], store_sem.at[level]
        )

    loads = [
        pltpu.make_async_copy(live, live_s, load_sem.at[0]),
        pltpu.make_async_copy(values, values_v, load_sem.at[1]),
        pltpu.make_async_copy(weights, weights_v, load_sem.at[2]),
        pltpu.make_async_copy(places, places_v, load_sem.at[3]),
        pltpu.make_async_copy(mask.at[0], sea_v, load_sem.at[4]),
        pltpu.make_async_copy(rows, rows_v, load_sem.at[5]),
        pltpu.make_async_copy(columns, columns_v, load_sem.at[6]),
    ]
    for load in loads:
        load.start()
    for level in range(levels):
        level_load(level).start()

    spare = packets * GROUP
    addends[:, spare : spare + GROUP] = jnp.zeros((12, GROUP, COLS), f32)
    total[...] = jnp.zeros_like(total)
    for at in range(spare + GROUP):
        order[at] = spare
    loads[0].wait()

    def list_packet(at, count):
        lines = (live_s[at, 0] + COLS - 1) // COLS

        def list_row(row, carry):
            order[count + row] = at * GROUP + row
            return carry

        lax.fori_loop(0, lines, list_row, 0)
        return count + lines

    live_lines = lax.fori_loop(0, jnp.where(is_ocean, packets, NEAR), list_packet, 0)

    for load in loads[1:3]:
        load.wait()

    def split_packets(group, carry):
        for n in range(NEAR):
            at = group * NEAR + n
            lines = pl.ds(pl.multiple_of(at * GROUP, GROUP), GROUP)
            weight = weights_v[lines] * 64.0
            for item in range(4):
                value = weight
                if item < 3:
                    value = weight * values_v[at, item * GROUP : (item + 1) * GROUP]
                for part in range(3):
                    piece = value.astype(f8).astype(f32)
                    addends[part * 4 + item, lines] = piece
                    value = (value - piece) * 16.0
        return carry

    lax.fori_loop(0, jnp.where(is_ocean, packets // NEAR, 1), split_packets, 0)
    for load in loads[3:]:
        load.wait()
    land[...] = 1.0 - sea_v[...].astype(jnp.float32)
    one = jnp.float32(1.0)
    zero = jnp.float32(0.0)
    valid_west = jnp.where(jnp.logical_or(is_ocean, ix > 0), one, zero)
    valid_east = jnp.where(jnp.logical_or(is_ocean, ix < count_x - 1), one, zero)
    valid_south = jnp.where(iy > 0, one, zero)
    valid_north = jnp.where(jnp.logical_or(is_ocean, iy < count_y - 1), one, zero)

    row_ids = lax.broadcasted_iota(jnp.int32, (ROWS, COLS), 0)
    col_ids = lax.broadcasted_iota(jnp.int32, (ROWS, COLS), 1)
    is_first_row = row_ids == 0
    is_last_row = row_ids == ROWS - 1
    is_first_col = col_ids == 0
    is_last_col = col_ids == COLS - 1
    ocean_share = jnp.where(is_ocean, one, zero)

    def before_x(field, edge):
        return jnp.where(is_first_row, edge, pltpu.roll(field, 1, 0))

    def after_x(field, edge):
        return jnp.where(is_last_row, edge, pltpu.roll(field, ROWS - 1, 0))

    def before_y(field, edge):
        return jnp.where(is_first_col, edge, pltpu.roll(field, 1, 1))

    def after_y(field, edge):
        return jnp.where(is_last_col, edge, pltpu.roll(field, COLS - 1, 1))

    def stencil(level):
        level_load(level).wait()
        pressure = fields[level, 0]
        zonal = fields[level, 1]
        meridional = fields[level, 2]
        tracer = fields[level, 3]
        half_wave = 0.5 * wave[0, level]
        drag = jnp.where(is_ocean, one, jnp.where(level == 0, gains[0, 2], zero))
        keeping = 1.0 - drag * land[...]
        tendency = 1.0 - ocean_share * land[...]
        edge_rows = [
            [rows_v[side, pl.ds(item * 8 + level, 1), :] for item in range(4)] for side in range(2)
        ]
        edge_cols = []
        for side in range(2):
            pairs = pltpu.roll(columns_v[side], lax.rem(128 - 2 * level, 128), 1)
            others = pltpu.roll(columns_v[side], lax.rem(128 - level, 128), 1)
            edge_cols.append(
                [
                    pairs[:, 1 - side : 2 - side],
                    pairs[:, side : side + 1],
                    others[:, 16:17],
                    others[:, 24:25],
                ]
            )
        row_keep = [
            (1.0 - drag * (1.0 - rows_v[0, 32:33, :])) * valid_west,
            (1.0 - drag * (1.0 - rows_v[1, 32:33, :])) * valid_east,
        ]
        col_keep = [
            (1.0 - drag * (1.0 - columns_v[0, :, 32:33])) * valid_south,
            (1.0 - drag * (1.0 - columns_v[1, :, 32:33])) * valid_north,
        ]
        new_zonal = keeping * (
            zonal
            - half_wave
            * (after_x(pressure, edge_rows[1][0]) - before_x(pressure, edge_rows[0][0]))
        )
        new_meridional = keeping * (
            meridional
            - half_wave
            * (after_y(pressure, edge_cols[1][0]) - before_y(pressure, edge_cols[0][0]))
        )
        zonal_west = row_keep[0] * (
            edge_rows[0][2] - half_wave * (pressure[0:1] - edge_rows[0][1])
        )
        zonal_east = row_keep[1] * (
            edge_rows[1][2] - half_wave * (edge_rows[1][1] - pressure[ROWS - 1 : ROWS])
        )
        meridional_south = col_keep[0] * (
            edge_cols[0][2] - half_wave * (pressure[:, 0:1] - edge_cols[0][1])
        )
        meridional_north = col_keep[1] * (
            edge_cols[1][2] - half_wave * (edge_cols[1][1] - pressure[:, COLS - 1 : COLS])
        )
        divergence = (
            after_x(new_zonal, zonal_east)
            - before_x(new_zonal, zonal_west)
            + after_y(new_meridional, meridional_north)
            - before_y(new_meridional, meridional_south)
        )
        laplace = (
            after_x(tracer, edge_rows[1][3])
            + before_x(tracer, edge_rows[0][3])
            + after_y(tracer, edge_cols[1][3])
            + before_y(tracer, edge_cols[0][3])
            - 4.0 * tracer
        )
        updated[level, 0] = pressure - half_wave * divergence
        updated[level, 1] = new_zonal
        updated[level, 2] = new_meridional
        updated[level, 3] = tracer + spread[0, level] * tendency * laplace

    narrow_ids = lax.broadcasted_iota(jnp.int16, (64, COLS), 0)
    wide_ids = lax.broadcasted_iota(jnp.int16, (2 * COLS, COLS), 0)
    one16 = jnp.ones((), jnp.bfloat16)
    zero16 = jnp.zeros((), jnp.bfloat16)

    def repeated(line, count, kind):
        tile = jnp.broadcast_to(line, (16, COLS)).astype(kind)
        return jnp.concatenate([tile] * (count // 16), axis=0)

    def scatter(batch, count):
        for at in range(count):
            line = pl.ds(order[batch * BATCH + at], 1)
            span = slice(at * COLS, (at + 1) * COLS)
            here = narrow_ids == repeated(places_v[0, line, :], 64, jnp.int16)
            for item in range(4):
                for part in range(3):
                    value = addends[part * 4 + item, line, :]
                    lead = (part * 4 + item) * 64
                    left[lead : lead + 64, span] = jnp.where(
                        here, repeated(value, 64, jnp.bfloat16), zero16
                    ).astype(f8)
            there = wide_ids == repeated(places_v[1, line, :], 2 * COLS, jnp.int16)
            right[:, span] = jnp.where(there, one16, zero16).astype(f8)
        total[...] += lax.dot_general(
            left[:, 0 : count * COLS],
            right[:, 0 : count * COLS],
            (((1,), (1,)), ((), ())),
            preferred_element_type=jnp.float32,
        )

    def level_step(level, carry):
        stencil(level)
        scatter(level, BATCH)

        @pl.when(level > 0)
        def _():
            level_store(level).start()

        return carry

    lax.fori_loop(0, levels, level_step, 0)

    def extra_step(batch, carry):
        scatter(batch, BATCH)
        return carry

    batches = levels + jnp.maximum(live_lines - levels * BATCH, 0) // BATCH
    rest = live_lines - batches * BATCH
    batches = jnp.where(rest > BATCH // 2, batches + 1, batches)
    lax.fori_loop(levels, batches, extra_step, 0)

    @pl.when(live_lines > batches * BATCH)
    def _():
        scatter(batches, BATCH // 2)

    for half in range(2):
        span = slice(half * 64, (half + 1) * 64)
        lanes = slice(half * COLS, (half + 1) * COLS)
        sums = [
            total[item * 64 : (item + 1) * 64, lanes] * (1.0 / 64.0)
            + total[256 + item * 64 : 256 + (item + 1) * 64, lanes] * (1.0 / 1024.0)
            + total[512 + item * 64 : 512 + (item + 1) * 64, lanes] * (1.0 / 16384.0)
            for item in range(4)
        ]
        tendency = 1.0 - ocean_share * land[span]
        for item, variable in enumerate((3, 1, 2)):
            gain = gains[0, 0] if variable == 3 else gains[0, 1]
            updated[0, variable, span] = updated[0, variable, span] + tendency * gain * (
                sums[item] - sums[3] * fields[0, variable, span]
            )
        first_store(half).start()
    for level in range(1, levels):
        level_store(level).wait()
    for half in range(2):
        first_store(half).wait()


def exchange_call(
    model_state, sea_mask, own_cells, target_cells, weight_ids, pair_counts, area_table, fold_map
):
    levels = model_state.shape[2]
    packets = (lax.axis_size("comp") - 1) * NEAR
    lines = packets * GROUP
    count_x = lax.axis_size("tx")
    anywhere = pl.BlockSpec(memory_space=pl.ANY)
    shapes = [
        ((2, lines + GROUP, COLS), i32),
        ((lines, COLS), f32),
        ((16, 128), i32),
        ((packets, 3 * GROUP, COLS), f32),
        ((2, 40, COLS), f32),
        ((2, ROWS, 128), f32),
    ]
    return pl.pallas_call(
        exchange_kernel,
        out_shape=tuple(jax.ShapeDtypeStruct(shape, kind) for shape, kind in shapes),
        in_specs=[pl.BlockSpec(memory_space=pltpu.SMEM)] + [anywhere] * 7,
        out_specs=[anywhere] * 6,
        scratch_shapes=[
            pltpu.VMEM((4, levels, ROWS, COLS), f32),
            pltpu.VMEM((ROWS, COLS), i32),
            pltpu.VMEM((NEAR, GROUP * COLS), i32),
            pltpu.VMEM((NEAR, GROUP * COLS), i32),
            pltpu.VMEM((NEAR, GROUP * COLS), i32),
            pltpu.VMEM(area_table.shape, f32),
            pltpu.VMEM((ROWS,), i32),
            pltpu.VMEM((3 * COLS, 2 * ROWS), jnp.bfloat16),
            pltpu.VMEM((NEAR, 2 * GROUP, COLS), i32),
            pltpu.VMEM((NEAR, 3 * GROUP, COLS), f32),
            pltpu.VMEM((2, 40, COLS), f32),
            pltpu.VMEM((2, ROWS, 128), f32),
            pltpu.VMEM((packets, 2 * GROUP, COLS), i32),
            pltpu.VMEM((2, lines + GROUP, COLS), i32),
            pltpu.VMEM((lines, COLS), f32),
            pltpu.VMEM((16, 128), i32),
            pltpu.VMEM((2, 40, COLS), f32),
            pltpu.VMEM((2, ROWS, 128), f32),
            pltpu.VMEM((count_x, ROWS, 128), f32),
            dma((8,)),
            dma((5,)),
            dma((packets,)),
            dma((packets,)),
            dma((packets,)),
            dma((packets,)),
            dma((4,)),
            dma((4,)),
            dma((count_x,)),
            dma((count_x,)),
        ],
        compiler_params=pltpu.CompilerParams(
            collective_id=0, has_side_effects=True, vmem_limit_bytes=60 * 2**20
        ),
        name="exchange",
    )(
        pair_counts,
        model_state,
        sea_mask,
        own_cells,
        target_cells,
        weight_ids,
        area_table,
        fold_map,
    )


def step_call(
    model_state,
    sea_mask,
    wave_speed,
    diffusivity,
    surface_gains,
    places,
    weights,
    live,
    values,
    rows,
    columns,
):
    levels = model_state.shape[2]
    lines = places.shape[1]
    anywhere = pl.BlockSpec(memory_space=pl.ANY)
    scalars = pl.BlockSpec(memory_space=pltpu.SMEM)
    return pl.pallas_call(
        step_kernel,
        out_shape=jax.ShapeDtypeStruct(model_state.shape, f32),
        in_specs=[scalars] * 3 + [anywhere] * 8,
        out_specs=anywhere,
        scratch_shapes=[
            pltpu.VMEM((levels, 4, ROWS, COLS), f32),
            pltpu.VMEM((levels, 4, ROWS, COLS), f32),
            pltpu.VMEM((ROWS, COLS), f32),
            pltpu.VMEM(places.shape, i32),
            pltpu.VMEM(weights.shape, f32),
            pltpu.VMEM(values.shape, f32),
            pltpu.VMEM(rows.shape, f32),
            pltpu.VMEM(columns.shape, f32),
            pltpu.VMEM((ROWS, COLS), i32),
            pltpu.VMEM((12, lines, COLS), f32),
            pltpu.SMEM(live.shape, i32),
            pltpu.SMEM((lines,), i32),
            pltpu.VMEM((3 * 4 * 64, BATCH * COLS), f8),
            pltpu.VMEM((2 * COLS, BATCH * COLS), f8),
            pltpu.VMEM((3 * 4 * 64, 2 * COLS), f32),
            dma((7,)),
            dma((levels,)),
            dma((levels + 1,)),
        ],
        compiler_params=pltpu.CompilerParams(vmem_limit_bytes=60 * 2**20),
        name="step",
    )(
        wave_speed,
        diffusivity,
        surface_gains,
        model_state,
        sea_mask,
        places,
        weights,
        live,
        values,
        rows,
        columns,
    )


def shards(
    model_state,
    sea_mask,
    wave_speed,
    diffusivity,
    surface_gains,
    area_table,
    own_cells,
    target_cells,
    weight_ids,
    pair_counts,
    fold_map,
):
    exchanged = exchange_call(
        model_state,
        sea_mask,
        own_cells,
        target_cells,
        weight_ids,
        pair_counts,
        area_table,
        fold_map,
    )
    return step_call(
        model_state, sea_mask, wave_speed, diffusivity, surface_gains, *exchanged
    )


def solution(mesh):
    in_specs = (
        P("comp", None, None, "tx", "ty"),
        P("comp", "tx", "ty"),
        P("comp", None),
        P("comp", None),
        P("comp", None),
        P(),
        P("comp", ("tx", "ty"), None, None),
        P("comp", ("tx", "ty"), None, None),
        P("comp", ("tx", "ty"), None, None),
        P("comp", ("tx", "ty"), None),
        P(),
    )
    out_specs = P("comp", None, None, "tx", "ty")
    return jax.shard_map(shards, mesh=mesh, in_specs=in_specs, out_specs=out_specs, check_vma=False)
```

```python
import jax
import jax.numpy as jnp
from jax import lax
from jax.experimental import pallas as pl
from jax.experimental.pallas import tpu as pltpu
from jax.sharding import PartitionSpec as P

MESH = pl.DeviceIdType.MESH
NEAR = 4
ROWS = 128
COLS = 256
f32 = jnp.float32
i32 = jnp.int32
f8 = jnp.float8_e4m3fn
dma = pltpu.SemaphoreType.DMA
GROUP = 8
PICK_UNROLL = 2
BATCH = 8


def exchange_kernel(
    counts,
    state,
    mask,
    own,
    target,
    ids,
    area,
    fold_map,
    places_out,
    weights_out,
    live_out,
    values_out,
    rows_out,
    columns_out,
    fields,
    sea,
    own_v,
    target_v,
    ids_v,
    area_v,
    fold_v,
    surface,
    early,
    late,
    rows_in,
    columns_in,
    arrived,
    places,
    weights,
    live,
    rows_got,
    columns_got,
    fold_got,
    load_sem,
    store_sem,
    early_send,
    early_recv,
    late_send,
    late_recv,
    edge_send,
    edge_recv,
    fold_send,
    fold_recv,
):
    levels = fields.shape[1]
    comps = lax.axis_size("comp")
    windows = comps - 1
    count_x = lax.axis_size("tx")
    count_y = lax.axis_size("ty")
    positions = count_x * count_y
    comp = lax.axis_index("comp")
    ix = lax.axis_index("tx")
    iy = lax.axis_index("ty")
    place = ix * count_y + iy
    is_ocean = comp == windows
    is_window = comp != windows
    on_fold = jnp.logical_and(is_ocean, iy == count_y - 1)
    offsets = [n % 2 + (n // 2) * count_y for n in range(NEAR)]

    def device_at(component, position):
        return (component, lax.div(position, count_y), lax.rem(position, count_y))

    loads = [
        pltpu.make_async_copy(target.at[0, 0], target_v, load_sem.at[0]),
        pltpu.make_async_copy(ids.at[0, 0], ids_v, load_sem.at[1]),
        pltpu.make_async_copy(own.at[0, 0], own_v, load_sem.at[2]),
        pltpu.make_async_copy(state.at[0, :, 0], fields.at[:, 0], load_sem.at[3]),
        pltpu.make_async_copy(
            state.at[0, :, pl.ds(1, levels - 1)], fields.at[:, pl.ds(1, levels - 1)], load_sem.at[4]
        ),
        pltpu.make_async_copy(mask.at[0], sea, load_sem.at[5]),
        pltpu.make_async_copy(area, area_v, load_sem.at[6]),
        pltpu.make_async_copy(fold_map.at[pl.ds(ix * ROWS, ROWS)], fold_v, load_sem.at[7]),
    ]
    for load in loads:
        load.start()

    west = (comp, lax.rem(ix + count_x - 1, count_x), iy)
    east = (comp, lax.rem(ix + 1, count_x), iy)
    south = (comp, ix, lax.rem(iy + count_y - 1, count_y))
    north = (comp, ix, lax.rem(iy + 1, count_y))

    barrier = pltpu.get_barrier_semaphore()
    for neighbour in (west, east, south, north):
        pl.semaphore_signal(barrier, inc=1, device_id=neighbour, device_id_type=MESH)
    sources = [lax.rem(place + positions - offset, positions) for offset in offsets]

    @pl.when(is_ocean)
    def _():
        for source in sources:
            for window in range(windows):
                pl.semaphore_signal(
                    barrier, inc=1, device_id=device_at(window, source), device_id_type=MESH
                )

    @pl.when(is_window)
    def _():
        for source in sources:
            pl.semaphore_signal(
                barrier, inc=1, device_id=device_at(windows, source), device_id_type=MESH
            )

    @pl.when(on_fold)
    def _():
        for step in range(1, count_x):
            pl.semaphore_signal(
                barrier,
                inc=1,
                device_id=(comp, lax.rem(ix + step, count_x), iy),
                device_id_type=MESH,
            )

    loads[0].wait()
    loads[1].wait()
    lane = lax.broadcasted_iota(jnp.int32, (1, COLS), 1)
    for n in range(NEAR):
        limit = counts[0, 0, n]
        for row in range(GROUP):
            span = slice(row * COLS, (row + 1) * COLS)
            cell = target_v[n : n + 1, span]
            early[n, row : row + 1] = jnp.where(lane + row * COLS < limit, cell, -1)
            early[n, GROUP + row : GROUP + row + 1] = ids_v[n : n + 1, span]

    slot = jnp.where(is_ocean, 0, comp * NEAR)

    def packet_copy(kind, n, window, component):
        position = lax.rem(place + offsets[n], positions)
        source, target_ref, send, recv = {
            "early": (early, arrived, early_send, early_recv),
            "late": (late, values_out, late_send, late_recv),
        }[kind]
        return pltpu.make_async_remote_copy(
            src_ref=source.at[n],
            dst_ref=target_ref.at[slot + n],
            send_sem=send.at[n * windows + window],
            recv_sem=recv.at[slot + n],
            device_id=device_at(component, position),
            device_id_type=MESH,
        )

    def send_packets(kind, n):
        @pl.when(is_ocean)
        def _():
            for window in range(windows):
                packet_copy(kind, n, window, window).start()

        @pl.when(is_window)
        def _():
            packet_copy(kind, n, 0, windows).start()

    loads[2].wait()
    loads[3].wait()
    for at, variable in enumerate((3, 1, 2)):
        turned = jnp.transpose(fields[variable, 0])
        high = turned.astype(jnp.bfloat16)
        low = (turned - high.astype(jnp.float32)).astype(jnp.bfloat16)
        surface[at * COLS : (at + 1) * COLS, 0:ROWS] = high
        surface[at * COLS : (at + 1) * COLS, ROWS : 2 * ROWS] = low

    row_ids = lax.broadcasted_iota(jnp.int32, (ROWS, COLS), 0)
    col_ids = lax.broadcasted_iota(jnp.int32, (COLS, COLS), 0)

    strip = ROWS // 2
    lanes = lax.broadcasted_iota(jnp.int32, (strip, 128), 1)

    def pack_strip(at, block):
        half = slice(at * 128, (at + 1) * 128)
        band = pl.ds(pl.multiple_of(block * strip, strip), strip)
        near, pair = (127, 126) if at else (0, 0)
        packed = jnp.where(
            lanes == 32,
            pltpu.roll(sea[band, half].astype(jnp.float32), (32 - near) % 128, 1),
            0.0,
        )
        for level in range(levels):
            turned = pltpu.roll(fields[0, level, band, half], (2 * level - pair) % 128, 1)
            packed = jnp.where((lanes >> 1) == level, turned, packed)
            for variable, first in ((2, 16), (3, 24)):
                turned = pltpu.roll(
                    fields[variable, level, band, half], (first + level - near) % 128, 1
                )
                packed = jnp.where(lanes == first + level, turned, packed)
        columns_in[at, band] = packed

    def pick(n, side):
        def pick_rows(part, carry):
            if side is not None:
                pack_strip(side, part)
            for step in range(GROUP // 2):
                row = part * (GROUP // 2) + step
                cell = own_v[n : n + 1, pl.ds(pl.multiple_of(row * COLS, COLS), COLS)]
                hot = jnp.where(row_ids == (cell >> 8), 1.0, 0.0).astype(jnp.bfloat16)
                chosen = jnp.dot(
                    surface[...],
                    jnp.concatenate([hot, hot], axis=0),
                    preferred_element_type=jnp.float32,
                )
                here = col_ids == (cell & (COLS - 1))
                for at in range(3):
                    part_of = jnp.where(here, chosen[at * COLS : (at + 1) * COLS], 0.0)
                    late[n, pl.ds(at * GROUP + row, 1), :] = jnp.sum(
                        part_of, axis=0, keepdims=True
                    )
            return carry

        lax.fori_loop(0, 2, pick_rows, 0, unroll=PICK_UNROLL)

    edge_copies = []
    for at, device in enumerate((west, east)):
        edge_copies.append(
            pltpu.make_async_remote_copy(
                src_ref=rows_in.at[at],
                dst_ref=rows_got.at[1 - at],
                send_sem=edge_send.at[at],
                recv_sem=edge_recv.at[1 - at],
                device_id=device,
                device_id_type=MESH,
            )
        )
    for at, device in enumerate((south, north)):
        edge_copies.append(
            pltpu.make_async_remote_copy(
                src_ref=columns_in.at[at],
                dst_ref=columns_got.at[1 - at],
                send_sem=edge_send.at[2 + at],
                recv_sem=edge_recv.at[2 + 1 - at],
                device_id=device,
                device_id_type=MESH,
            )
        )

    def fold_copy(step):
        return pltpu.make_async_remote_copy(
            src_ref=columns_in.at[1],
            dst_ref=fold_got.at[ix],
            send_sem=fold_send.at[step],
            recv_sem=fold_recv.at[step],
            device_id=(comp, lax.rem(ix + step, count_x), iy),
            device_id_type=MESH,
        )

    fold_keep = pltpu.make_async_copy(columns_in.at[1], fold_got.at[ix], fold_send.at[0])

    def send_edges():
        for at, (near, far) in enumerate(((0, 1), (ROWS - 1, ROWS - 2))):
            for level in range(levels):
                for item, (variable, row) in enumerate(((0, near), (0, far), (1, near), (3, near))):
                    rows_in[at, item * 8 + level : item * 8 + level + 1] = fields[
                        variable, level, row : row + 1, :
                    ]
            rows_in[at, 32:33] = sea[near : near + 1].astype(jnp.float32)
        for copy in edge_copies:
            copy.start()

        @pl.when(on_fold)
        def _():
            fold_keep.start()
            for step in range(1, count_x):
                fold_copy(step).start()

    pick(3, None)
    @pl.when(is_window)
    def _():
        pl.semaphore_wait(barrier, 4 + NEAR)

    @pl.when(jnp.logical_and(is_ocean, iy != count_y - 1))
    def _():
        pl.semaphore_wait(barrier, 4 + windows * NEAR)

    @pl.when(on_fold)
    def _():
        pl.semaphore_wait(barrier, 4 + windows * NEAR + count_x - 1)

    for n in reversed(range(NEAR)):
        send_packets("early", n)

    send_packets("late", 3)
    loads[4].wait()
    loads[5].wait()
    pick(2, 0)
    send_packets("late", 2)
    pick(1, 1)
    send_packets("late", 1)
    send_edges()
    pick(0, None)
    send_packets("late", 0)

    def wait_slot(kind, at):
        target_ref, recv, source = {
            "early": (arrived, early_recv, early),
            "late": (values_out, late_recv, late),
        }[kind]
        pltpu.make_async_remote_copy(
            src_ref=source.at[0],
            dst_ref=target_ref.at[at],
            send_sem=early_send.at[0],
            recv_sem=recv.at[at],
            device_id=west,
            device_id_type=MESH,
        ).wait_recv()

    def finish(kind):
        @pl.when(is_ocean)
        def _():
            for n in range(NEAR):
                for window in range(windows):
                    packet_copy(kind, n, window, window).wait_send()
            for at in range(windows * NEAR):
                wait_slot(kind, at)

        @pl.when(is_window)
        def _():
            for n in range(NEAR):
                packet_copy(kind, n, 0, windows).wait_send()
            for at in range(NEAR):
                wait_slot(kind, at)

    loads[6].wait()
    loads[7].wait()
    spare = windows * NEAR * GROUP
    places[0, spare : spare + GROUP] = jnp.zeros((GROUP, COLS), i32)
    places[1, spare : spare + GROUP] = jnp.full((GROUP, COLS), -1, i32)
    table = [
        jnp.broadcast_to(area_v[at * 128 : (at + 1) * 128][None], (GROUP, 128)) for at in range(2)
    ]
    slot_ids = lax.broadcasted_iota(
        jnp.int32, (GROUP, COLS), 0
    ) * COLS + lax.broadcasted_iota(jnp.int32, (GROUP, COLS), 1)
    mine = jnp.logical_or(slot_ids - 3 * ((slot_ids * 43691) >> 17) == comp, is_ocean)
    finish("early")

    def place_packets(group, carry):
        for n in range(NEAR):
            at = group * NEAR + n
            cell = arrived[at, 0:GROUP]
            entry = arrived[at, GROUP : 2 * GROUP]
            lines = pl.ds(pl.multiple_of(at * GROUP, GROUP), GROUP)
            for half in range(2):
                span = slice(half * 128, (half + 1) * 128)
                index = entry[:, span]
                low = jnp.take_along_axis(table[0], index & 127, axis=1, mode="promise_in_bounds")
                high = jnp.take_along_axis(table[1], index & 127, axis=1, mode="promise_in_bounds")
                weights[lines, span] = jnp.where(index < 128, low, high)
            row = cell >> 8
            places[0, lines] = row & 63
            alive = jnp.logical_and(cell >= 0, mine)
            places[1, lines] = jnp.where(alive, ((row >> 6) << 8) + (cell & (COLS - 1)), -1)
            used = jnp.sum(jnp.where(cell >= 0, 1.0, 0.0), axis=0, keepdims=True)
            used = jnp.sum(used, axis=1, keepdims=True)
            live[pl.ds(at, 1)] = jnp.broadcast_to(used, (1, 128)).astype(jnp.int32)
        return carry

    lax.fori_loop(0, jnp.where(is_ocean, windows, 1), place_packets, 0)
    stores = [
        pltpu.make_async_copy(places, places_out, store_sem.at[0]),
        pltpu.make_async_copy(weights, weights_out, store_sem.at[1]),
        pltpu.make_async_copy(live, live_out, store_sem.at[2]),
        pltpu.make_async_copy(rows_got, rows_out, store_sem.at[3]),
        pltpu.make_async_copy(columns_got, columns_out, store_sem.at[4]),
    ]
    for store in stores[:3]:
        store.start()

    for copy in edge_copies:
        copy.wait_send()
        copy.wait_recv()
    one = jnp.float32(1.0)
    zero = jnp.float32(0.0)
    rows_got[0] = rows_got[0] * jnp.where(jnp.logical_or(is_ocean, ix > 0), one, zero)
    rows_got[1] = rows_got[1] * jnp.where(jnp.logical_or(is_ocean, ix < count_x - 1), one, zero)
    columns_got[0] = columns_got[0] * jnp.where(iy > 0, one, zero)
    columns_got[1] = columns_got[1] * jnp.where(iy < count_y - 1, one, zero)

    @pl.when(on_fold)
    def _():
        fold_keep.wait()
        for step in range(1, count_x):
            fold_copy(step).wait_send()
            fold_copy(step).wait_recv()
        wanted = jnp.transpose(jnp.broadcast_to(fold_v[...][None], (ROWS, ROWS)))
        lanes = lax.broadcasted_iota(jnp.int32, (ROWS, 128), 1)
        gathered = jnp.zeros((ROWS, 128), f32)
        for block in range(count_x):
            hot = jnp.where(wanted == lanes + block * ROWS, 1.0, 0.0).astype(jnp.bfloat16)
            rest = fold_got[block]
            for part in range(3):
                piece = rest.astype(jnp.bfloat16)
                rest = rest - piece.astype(f32)
                gathered += jnp.dot(hot, piece, preferred_element_type=f32)
        swapped = jnp.where(
            (lanes & 1) == 0, pltpu.roll(gathered, 127, 1), pltpu.roll(gathered, 1, 1)
        )
        gathered = jnp.where(lanes < 16, swapped, gathered)
        turned = jnp.logical_and(lanes >= 16, lanes < 24)
        columns_got[1] = jnp.where(turned, -gathered, gathered)

    for store in stores[3:]:
        store.start()
    finish("late")
    for store in stores:
        store.wait()


def step_kernel(
    wave,
    spread,
    gains,
    state,
    mask,
    places,
    weights,
    live,
    values,
    rows,
    columns,
    result,
    fields,
    updated,
    land,
    places_v,
    weights_v,
    values_v,
    rows_v,
    columns_v,
    sea_v,
    addends,
    live_s,
    order,
    left,
    right,
    total,
    load_sem,
    level_sem,
    store_sem,
):
    levels = fields.shape[0]
    windows = lax.axis_size("comp") - 1
    count_x = lax.axis_size("tx")
    count_y = lax.axis_size("ty")
    comp = lax.axis_index("comp")
    ix = lax.axis_index("tx")
    iy = lax.axis_index("ty")
    is_ocean = comp == windows
    packets = values_v.shape[0]

    def level_load(level):
        return pltpu.make_async_copy(state.at[0, :, level], fields.at[level], level_sem.at[level])

    def first_store(half):
        span = pl.ds(half * 64, 64)
        return pltpu.make_async_copy(
            updated.at[0, :, span], result.at[0, :, 0, span], store_sem.at[half * levels]
        )

    def level_store(level):
        return pltpu.make_async_copy(
            updated.at[level], result.at[0, :, level], store_sem.at[level]
        )

    loads = [
        pltpu.make_async_copy(live, live_s, load_sem.at[0]),
        pltpu.make_async_copy(values, values_v, load_sem.at[1]),
        pltpu.make_async_copy(weights, weights_v, load_sem.at[2]),
        pltpu.make_async_copy(places, places_v, load_sem.at[3]),
        pltpu.make_async_copy(mask.at[0], sea_v, load_sem.at[4]),
        pltpu.make_async_copy(rows, rows_v, load_sem.at[5]),
        pltpu.make_async_copy(columns, columns_v, load_sem.at[6]),
    ]
    for load in loads:
        load.start()
    for level in range(levels):
        level_load(level).start()

    spare = packets * GROUP
    addends[:, spare : spare + GROUP] = jnp.zeros((12, GROUP, COLS), f32)
    total[...] = jnp.zeros_like(total)
    for at in range(spare + GROUP):
        order[at] = spare
    loads[0].wait()

    def list_packet(at, count):
        lines = (live_s[at, 0] + COLS - 1) // COLS

        def list_row(row, carry):
            order[count + row] = at * GROUP + row
            return carry

        lax.fori_loop(0, lines, list_row, 0)
        return count + lines

    live_lines = lax.fori_loop(0, jnp.where(is_ocean, packets, NEAR), list_packet, 0)

    for load in loads[1:3]:
        load.wait()

    def split_packets(group, carry):
        for n in range(NEAR):
            at = group * NEAR + n
            lines = pl.ds(pl.multiple_of(at * GROUP, GROUP), GROUP)
            weight = weights_v[lines] * 64.0
            for item in range(4):
                value = weight
                if item < 3:
                    value = weight * values_v[at, item * GROUP : (item + 1) * GROUP]
                for part in range(3):
                    piece = value.astype(f8).astype(f32)
                    addends[part * 4 + item, lines] = piece
                    value = (value - piece) * 16.0
        return carry

    lax.fori_loop(0, jnp.where(is_ocean, packets // NEAR, 1), split_packets, 0)
    for load in loads[3:]:
        load.wait()
    land[...] = 1.0 - sea_v[...].astype(jnp.float32)
    one = jnp.float32(1.0)
    zero = jnp.float32(0.0)
    valid_west = jnp.where(jnp.logical_or(is_ocean, ix > 0), one, zero)
    valid_east = jnp.where(jnp.logical_or(is_ocean, ix < count_x - 1), one, zero)
    valid_south = jnp.where(iy > 0, one, zero)
    valid_north = jnp.where(jnp.logical_or(is_ocean, iy < count_y - 1), one, zero)

    row_ids = lax.broadcasted_iota(jnp.int32, (ROWS, COLS), 0)
    col_ids = lax.broadcasted_iota(jnp.int32, (ROWS, COLS), 1)
    is_first_row = row_ids == 0
    is_last_row = row_ids == ROWS - 1
    is_first_col = col_ids == 0
    is_last_col = col_ids == COLS - 1
    ocean_share = jnp.where(is_ocean, one, zero)

    def before_x(field, edge):
        return jnp.where(is_first_row, edge, pltpu.roll(field, 1, 0))

    def after_x(field, edge):
        return jnp.where(is_last_row, edge, pltpu.roll(field, ROWS - 1, 0))

    def before_y(field, edge):
        return jnp.where(is_first_col, edge, pltpu.roll(field, 1, 1))

    def after_y(field, edge):
        return jnp.where(is_last_col, edge, pltpu.roll(field, COLS - 1, 1))

    def stencil(level):
        level_load(level).wait()
        pressure = fields[level, 0]
        zonal = fields[level, 1]
        meridional = fields[level, 2]
        tracer = fields[level, 3]
        half_wave = 0.5 * wave[0, level]
        drag = jnp.where(is_ocean, one, jnp.where(level == 0, gains[0, 2], zero))
        keeping = 1.0 - drag * land[...]
        tendency = 1.0 - ocean_share * land[...]
        edge_rows = [
            [rows_v[side, pl.ds(item * 8 + level, 1), :] for item in range(4)] for side in range(2)
        ]
        edge_cols = []
        for side in range(2):
            pairs = pltpu.roll(columns_v[side], lax.rem(128 - 2 * level, 128), 1)
            others = pltpu.roll(columns_v[side], lax.rem(128 - level, 128), 1)
            edge_cols.append(
                [
                    pairs[:, 1 - side : 2 - side],
                    pairs[:, side : side + 1],
                    others[:, 16:17],
                    others[:, 24:25],
                ]
            )
        row_keep = [
            (1.0 - drag * (1.0 - rows_v[0, 32:33, :])) * valid_west,
            (1.0 - drag * (1.0 - rows_v[1, 32:33, :])) * valid_east,
        ]
        col_keep = [
            (1.0 - drag * (1.0 - columns_v[0, :, 32:33])) * valid_south,
            (1.0 - drag * (1.0 - columns_v[1, :, 32:33])) * valid_north,
        ]
        new_zonal = keeping * (
            zonal
            - half_wave
            * (after_x(pressure, edge_rows[1][0]) - before_x(pressure, edge_rows[0][0]))
        )
        new_meridional = keeping * (
            meridional
            - half_wave
            * (after_y(pressure, edge_cols[1][0]) - before_y(pressure, edge_cols[0][0]))
        )
        zonal_west = row_keep[0] * (
            edge_rows[0][2] - half_wave * (pressure[0:1] - edge_rows[0][1])
        )
        zonal_east = row_keep[1] * (
            edge_rows[1][2] - half_wave * (edge_rows[1][1] - pressure[ROWS - 1 : ROWS])
        )
        meridional_south = col_keep[0] * (
            edge_cols[0][2] - half_wave * (pressure[:, 0:1] - edge_cols[0][1])
        )
        meridional_north = col_keep[1] * (
            edge_cols[1][2] - half_wave * (edge_cols[1][1] - pressure[:, COLS - 1 : COLS])
        )
        divergence = (
            after_x(new_zonal, zonal_east)
            - before_x(new_zonal, zonal_west)
            + after_y(new_meridional, meridional_north)
            - before_y(new_meridional, meridional_south)
        )
        laplace = (
            after_x(tracer, edge_rows[1][3])
            + before_x(tracer, edge_rows[0][3])
            + after_y(tracer, edge_cols[1][3])
            + before_y(tracer, edge_cols[0][3])
            - 4.0 * tracer
        )
        updated[level, 0] = pressure - half_wave * divergence
        updated[level, 1] = new_zonal
        updated[level, 2] = new_meridional
        updated[level, 3] = tracer + spread[0, level] * tendency * laplace

    narrow_ids = lax.broadcasted_iota(jnp.int16, (64, COLS), 0)
    wide_ids = lax.broadcasted_iota(jnp.int16, (2 * COLS, COLS), 0)
    one16 = jnp.ones((), jnp.bfloat16)
    zero16 = jnp.zeros((), jnp.bfloat16)

    def repeated(line, count, kind):
        tile = jnp.broadcast_to(line, (16, COLS)).astype(kind)
        return jnp.concatenate([tile] * (count // 16), axis=0)

    def scatter(batch, count):
        for at in range(count):
            line = pl.ds(order[batch * BATCH + at], 1)
            span = slice(at * COLS, (at + 1) * COLS)
            here = narrow_ids == repeated(places_v[0, line, :], 64, jnp.int16)
            for item in range(4):
                for part in range(3):
                    value = addends[part * 4 + item, line, :]
                    lead = (part * 4 + item) * 64
                    left[lead : lead + 64, span] = jnp.where(
                        here, repeated(value, 64, jnp.bfloat16), zero16
                    ).astype(f8)
            there = wide_ids == repeated(places_v[1, line, :], 2 * COLS, jnp.int16)
            right[:, span] = jnp.where(there, one16, zero16).astype(f8)
        total[...] += lax.dot_general(
            left[:, 0 : count * COLS],
            right[:, 0 : count * COLS],
            (((1,), (1,)), ((), ())),
            preferred_element_type=jnp.float32,
        )

    def level_step(level, carry):
        stencil(level)
        scatter(level, BATCH)

        @pl.when(level > 0)
        def _():
            level_store(level).start()

        return carry

    lax.fori_loop(0, levels, level_step, 0)

    def extra_step(batch, carry):
        scatter(batch, BATCH)
        return carry

    batches = levels + jnp.maximum(live_lines - levels * BATCH, 0) // BATCH
    rest = live_lines - batches * BATCH
    batches = jnp.where(rest > BATCH - 2, batches + 1, batches)
    lax.fori_loop(levels, batches, extra_step, 0)
    rest = live_lines - batches * BATCH
    for count in range(2, BATCH, 2):

        @pl.when(jnp.logical_and(rest > count - 2, rest <= count))
        def _():
            scatter(batches, count)

    for half in range(2):
        span = slice(half * 64, (half + 1) * 64)
        lanes = slice(half * COLS, (half + 1) * COLS)
        sums = [
            total[item * 64 : (item + 1) * 64, lanes] * (1.0 / 64.0)
            + total[256 + item * 64 : 256 + (item + 1) * 64, lanes] * (1.0 / 1024.0)
            + total[512 + item * 64 : 512 + (item + 1) * 64, lanes] * (1.0 / 16384.0)
            for item in range(4)
        ]
        tendency = 1.0 - ocean_share * land[span]
        for item, variable in enumerate((3, 1, 2)):
            gain = gains[0, 0] if variable == 3 else gains[0, 1]
            updated[0, variable, span] = updated[0, variable, span] + tendency * gain * (
                sums[item] - sums[3] * fields[0, variable, span]
            )
        first_store(half).start()
    for level in range(1, levels):
        level_store(level).wait()
    for half in range(2):
        first_store(half).wait()


def exchange_call(
    model_state, sea_mask, own_cells, target_cells, weight_ids, pair_counts, area_table, fold_map
):
    levels = model_state.shape[2]
    packets = (lax.axis_size("comp") - 1) * NEAR
    lines = packets * GROUP
    count_x = lax.axis_size("tx")
    anywhere = pl.BlockSpec(memory_space=pl.ANY)
    shapes = [
        ((2, lines + GROUP, COLS), i32),
        ((lines, COLS), f32),
        ((16, 128), i32),
        ((packets, 3 * GROUP, COLS), f32),
        ((2, 40, COLS), f32),
        ((2, ROWS, 128), f32),
    ]
    return pl.pallas_call(
        exchange_kernel,
        out_shape=tuple(jax.ShapeDtypeStruct(shape, kind) for shape, kind in shapes),
        in_specs=[pl.BlockSpec(memory_space=pltpu.SMEM)] + [anywhere] * 7,
        out_specs=[anywhere] * 6,
        scratch_shapes=[
            pltpu.VMEM((4, levels, ROWS, COLS), f32),
            pltpu.VMEM((ROWS, COLS), i32),
            pltpu.VMEM((NEAR, GROUP * COLS), i32),
            pltpu.VMEM((NEAR, GROUP * COLS), i32),
            pltpu.VMEM((NEAR, GROUP * COLS), i32),
            pltpu.VMEM(area_table.shape, f32),
            pltpu.VMEM((ROWS,), i32),
            pltpu.VMEM((3 * COLS, 2 * ROWS), jnp.bfloat16),
            pltpu.VMEM((NEAR, 2 * GROUP, COLS), i32),
            pltpu.VMEM((NEAR, 3 * GROUP, COLS), f32),
            pltpu.VMEM((2, 40, COLS), f32),
            pltpu.VMEM((2, ROWS, 128), f32),
            pltpu.VMEM((packets, 2 * GROUP, COLS), i32),
            pltpu.VMEM((2, lines + GROUP, COLS), i32),
            pltpu.VMEM((lines, COLS), f32),
            pltpu.VMEM((16, 128), i32),
            pltpu.VMEM((2, 40, COLS), f32),
            pltpu.VMEM((2, ROWS, 128), f32),
            pltpu.VMEM((count_x, ROWS, 128), f32),
            dma((8,)),
            dma((5,)),
            dma((packets,)),
            dma((packets,)),
            dma((packets,)),
            dma((packets,)),
            dma((4,)),
            dma((4,)),
            dma((count_x,)),
            dma((count_x,)),
        ],
        compiler_params=pltpu.CompilerParams(
            collective_id=0, has_side_effects=True, vmem_limit_bytes=60 * 2**20
        ),
        name="exchange",
    )(
        pair_counts,
        model_state,
        sea_mask,
        own_cells,
        target_cells,
        weight_ids,
        area_table,
        fold_map,
    )


def step_call(
    model_state,
    sea_mask,
    wave_speed,
    diffusivity,
    surface_gains,
    places,
    weights,
    live,
    values,
    rows,
    columns,
):
    levels = model_state.shape[2]
    lines = places.shape[1]
    anywhere = pl.BlockSpec(memory_space=pl.ANY)
    scalars = pl.BlockSpec(memory_space=pltpu.SMEM)
    return pl.pallas_call(
        step_kernel,
        out_shape=jax.ShapeDtypeStruct(model_state.shape, f32),
        in_specs=[scalars] * 3 + [anywhere] * 8,
        out_specs=anywhere,
        scratch_shapes=[
            pltpu.VMEM((levels, 4, ROWS, COLS), f32),
            pltpu.VMEM((levels, 4, ROWS, COLS), f32),
            pltpu.VMEM((ROWS, COLS), f32),
            pltpu.VMEM(places.shape, i32),
            pltpu.VMEM(weights.shape, f32),
            pltpu.VMEM(values.shape, f32),
            pltpu.VMEM(rows.shape, f32),
            pltpu.VMEM(columns.shape, f32),
            pltpu.VMEM((ROWS, COLS), i32),
            pltpu.VMEM((12, lines, COLS), f32),
            pltpu.SMEM(live.shape, i32),
            pltpu.SMEM((lines,), i32),
            pltpu.VMEM((3 * 4 * 64, BATCH * COLS), f8),
            pltpu.VMEM((2 * COLS, BATCH * COLS), f8),
            pltpu.VMEM((3 * 4 * 64, 2 * COLS), f32),
            dma((7,)),
            dma((levels,)),
            dma((levels + 1,)),
        ],
        compiler_params=pltpu.CompilerParams(vmem_limit_bytes=60 * 2**20),
        name="step",
    )(
        wave_speed,
        diffusivity,
        surface_gains,
        model_state,
        sea_mask,
        places,
        weights,
        live,
        values,
        rows,
        columns,
    )


def shards(
    model_state,
    sea_mask,
    wave_speed,
    diffusivity,
    surface_gains,
    area_table,
    own_cells,
    target_cells,
    weight_ids,
    pair_counts,
    fold_map,
):
    exchanged = exchange_call(
        model_state,
        sea_mask,
        own_cells,
        target_cells,
        weight_ids,
        pair_counts,
        area_table,
        fold_map,
    )
    return step_call(
        model_state, sea_mask, wave_speed, diffusivity, surface_gains, *exchanged
    )


def solution(mesh):
    in_specs = (
        P("comp", None, None, "tx", "ty"),
        P("comp", "tx", "ty"),
        P("comp", None),
        P("comp", None),
        P("comp", None),
        P(),
        P("comp", ("tx", "ty"), None, None),
        P("comp", ("tx", "ty"), None, None),
        P("comp", ("tx", "ty"), None, None),
        P("comp", ("tx", "ty"), None),
        P(),
    )
    out_specs = P("comp", None, None, "tx", "ty")
    return jax.shard_map(shards, mesh=mesh, in_specs=in_specs, out_specs=out_specs, check_vma=False)
```
